32 devices in a mesh: wide: 8 (over y, x, core), narrow: 4 (over z).
Axes of the slice: x: 2, y: 2, z: 4, core: 2. Of those that a mesh axis runs over, the one named last changes fastest.
Arguments:
- tokens: bfloat16 [16384, 768], P(('wide', 'narrow')), may hold values from -6 to 6
- block_size: int32 [8], P('wide'), may hold values from 4 to 16, as said below
- ln1_gain: bfloat16 [768], replicated, may hold values from 0.5 to 1.5
- ln1_shift: bfloat16 [768], replicated, may hold values from -1.5 to 1.5
- qkv_weight: bfloat16 [768, 3, 768], P(None, None, 'narrow'), may hold values from -0.21875 to 0.21875
- qkv_bias: bfloat16 [3, 768], P(None, 'narrow'), may hold values from -1.5 to 1.5
- out_weight: bfloat16 [768, 768], P('narrow'), may hold values from -1.75 to 1.75
- out_bias: bfloat16 [768], replicated, may hold values from -1.5 to 1.5
- ln2_gain: bfloat16 [768], replicated, may hold values from 0.5 to 1.5
- ln2_shift: bfloat16 [768], replicated, may hold values from -1.5 to 1.5
- up_weight: bfloat16 [768, 3072], P(None, 'narrow'), may hold values from -0.21875 to 0.21875
- up_bias: bfloat16 [3072], P('narrow'), may hold values from -1.5 to 1.5
- down_weight: bfloat16 [3072, 768], P('narrow'), may hold values from -0.109375 to 0.109375
- down_bias: bfloat16 [768], replicated, may hold values from -1.5 to 1.5
- cotangent: bfloat16 [16384, 768], P(('wide', 'narrow')), may hold values from -6 to 6
Outputs:
- activations: bfloat16 [16384, 768], P(('wide', 'narrow'))
- tokens_grad: bfloat16 [16384, 768], P(('wide', 'narrow'))
- grad_ln1_gain: float32 [768], replicated
- grad_ln1_shift: float32 [768], replicated
- grad_qkv_weight: float32 [768, 3, 768], P(None, None, 'narrow')
- grad_qkv_bias: float32 [3, 768], P(None, 'narrow')
- grad_out_weight: float32 [768, 768], P('narrow')
- grad_out_bias: float32 [768], replicated
- grad_ln2_gain: float32 [768], replicated
- grad_ln2_shift: float32 [768], replicated
- grad_up_weight: float32 [768, 3072], P(None, 'narrow')
- grad_up_bias: float32 [3072], P('narrow')
- grad_down_weight: float32 [3072, 768], P('narrow')
- grad_down_bias: float32 [768], replicated
The draws below stay inside these ranges and needn't reach their ends.
Inputs may be any that keep to these rules, and one draw needn't show every extreme that they name: `block_size`: each sequence's block size is 4, 8 or 16, and each of the three is some sequence's.
All inputs are finite; a program needn't handle non-finite values.
Results may differ from the reference program's by a relative error of at most 0.02.
Values may be sent and summed in bfloat16 or wider, within the bound.
A program may use at most 192 MiB of HBM per device.

```python
import math
import jax
import jax.numpy as jnp
from jax import lax

D = 768
HEADS = 12
HEAD_DIM = 64
FF = 3072
SEQ = 2048
SEQUENCES = 8
TOKENS = 16384


def draw_block_size(key, part):
    order = jax.random.permutation(key, SEQUENCES).astype(jnp.int32)
    residue = order % 3
    sizes = jnp.where(residue == 0, 4, jnp.where(residue == 1, 8, 16))
    return sizes.astype(jnp.int32)


def levels(own_key, shape, cuts, low, high):
    def one(position, blocks):
        steps = jax.random.uniform(jax.random.fold_in(jax.random.fold_in(own_key, 6), position), (blocks,), jnp.float32, low / len(cuts), high / len(cuts))
        return jnp.repeat(jnp.exp(steps), shape[position] // blocks).reshape((-1,) + (1,) * (len(shape) - position - 1))

    gain = one(*cuts[0])
    for cut in cuts[1:]:
        gain = gain * one(*cut)
    return gain


def gaussian(rng, shape, width, limit, split=(), kind=jnp.bfloat16):
    drawn = jax.random.normal(rng, shape, jnp.float32) * width
    if len(split) > 0:
        drawn = levels(rng, shape, split, -0.22, 0.18) * drawn
    return jnp.clip(drawn, min=-limit, max=limit).astype(kind)


def setup_inputs(seed: int = 0) -> dict:
    keys = jax.random.split(jax.random.key(seed), 16)
    return {
        "tokens": gaussian(keys[0], (TOKENS, D), 1.0, 6.0, ((0, 32),)),
        "block_size": draw_block_size(jax.random.fold_in(keys[15], 71), 0),
        "ln1_gain": jnp.clip(1.0 + 0.1 * jax.random.normal(keys[2], (D,), jnp.float32), 0.5, 1.5).astype(jnp.bfloat16),
        "ln1_shift": gaussian(keys[3], (D,), 0.3, 1.5),
        "qkv_weight": gaussian(keys[4], (D, 3, D), D ** -0.5, 0.21875, ((2, 4),)),
        "qkv_bias": gaussian(keys[5], (3, D), 0.3, 1.5, ((1, 4),)),
        "out_weight": gaussian(keys[6], (D, D), (D // 64) ** -0.5, 1.75, ((0, 4),)),
        "out_bias": gaussian(keys[7], (D,), 0.3, 1.5),
        "ln2_gain": jnp.clip(1.0 + 0.1 * jax.random.normal(keys[8], (D,), jnp.float32), 0.5, 1.5).astype(jnp.bfloat16),
        "ln2_shift": gaussian(keys[9], (D,), 0.3, 1.5),
        "up_weight": gaussian(keys[10], (D, FF), D ** -0.5, 0.21875, ((1, 4),)),
        "up_bias": gaussian(keys[11], (FF,), 0.3, 1.5, ((0, 4),)),
        "down_weight": gaussian(keys[12], (FF, D), FF ** -0.5, 0.109375, ((0, 4),)),
        "down_bias": gaussian(keys[13], (D,), 0.3, 1.5),
        "cotangent": gaussian(keys[14], (TOKENS, D), 1.0, 6.0, ((0, 32),)),
    }


highest = lax.Precision.HIGHEST
masked_value = -1e+30

@jax.custom_vjp
def low(v):
    return lax.optimization_barrier(v.astype(jnp.bfloat16)).astype(jnp.float32)

@jax.custom_vjp
def low_back(v):
    return v

def low_keep(v):
    return (low(v), None)

def low_pass(kept, grad):
    return (grad,)

def back_keep(v):
    return (v, None)

def back_low(kept, grad):
    return (low(grad),)
low.defvjp(low_keep, low_pass)
low_back.defvjp(back_keep, back_low)

def layer_norm(residual, norm_gain, norm_shift):
    row_mean = lax.optimization_barrier(jnp.mean(residual, axis=-1, keepdims=True))
    centered = residual - row_mean
    variance = lax.optimization_barrier(jnp.mean(centered * centered, axis=-1, keepdims=True))
    return centered * lax.rsqrt(variance + 1e-05) * norm_gain + norm_shift

def angle_tables(seq_len):
    half_len = seq_len // 2
    places = (jnp.arange(seq_len, dtype=jnp.int32) % half_len).astype(jnp.float32)
    freqs = jnp.exp(jnp.arange(HEAD_DIM // 2, dtype=jnp.int32).astype(jnp.float32) * (-2.0 * math.log(10000.0) / HEAD_DIM))
    angles = places[:, None] * freqs[None, :]
    return (jnp.cos(angles)[:, None, :], jnp.sin(angles)[:, None, :])

def rotate(features, cosine, sine_table):
    half_dim = features.shape[-1] // 2
    first = features[..., :half_dim]
    second = features[..., half_dim:]
    return jnp.concatenate([first * cosine - second * sine_table, second * cosine + first * sine_table], axis=-1)

def allowed_pairs(row_index, seq_len, block_len):
    half_len = seq_len // 2
    col_index = jnp.arange(seq_len, dtype=jnp.int32)
    row_clean = (row_index >= half_len)[:, None]
    col_clean = (col_index >= half_len)[None, :]
    row_noisy = jnp.logical_not(row_clean)
    col_noisy = jnp.logical_not(col_clean)
    row_block = (row_index % half_len // block_len)[:, None]
    col_block = (col_index % half_len // block_len)[None, :]
    same_block = row_noisy & col_noisy & (row_block == col_block)
    earlier = row_noisy & col_clean & (col_block < row_block)
    causal = row_clean & col_clean & (col_block <= row_block)
    return same_block | earlier | causal

def attention(queries, key_rows, values, block_len):
    seq_len = queries.shape[0]
    span_rows = min(512, seq_len)
    block_count = seq_len // span_rows
    score_scale = HEAD_DIM ** (-0.5)

    @jax.checkpoint
    def one_block(start_row):
        query_part = lax.dynamic_slice_in_dim(queries, start_row, span_rows, 0)
        row_index = start_row + jnp.arange(span_rows, dtype=jnp.int32)
        scores = low_back(jnp.einsum('qhe,khe->hqk', query_part, key_rows, precision=highest) * score_scale)
        scores = jnp.where(allowed_pairs(row_index, seq_len, block_len)[None], scores, masked_value)
        row_top = lax.optimization_barrier(jnp.max(scores, axis=-1, keepdims=True))
        expos = jnp.exp(scores - row_top)
        probs = expos / lax.optimization_barrier(jnp.sum(expos, axis=-1, keepdims=True))
        return jnp.einsum('hqk,khe->qhe', low(probs), values, precision=highest)
    starts = jnp.arange(block_count, dtype=jnp.int32) * span_rows
    blocks_out = lax.map(one_block, starts)
    return blocks_out.reshape(queries.shape)

def forward(residual, params, block_len):
    first_gain, first_shift, qkv_weight, qkv_bias, out_weight, out_bias, second_gain, second_shift, up_weight, up_bias, down_weight, down_bias = params
    seq_len = residual.shape[0]
    act1 = low(layer_norm(residual, first_gain, first_shift))
    proj = low_back(jnp.dot(act1, qkv_weight.reshape(D, 3 * D), precision=highest) + qkv_bias.reshape(3 * D))
    proj = proj.reshape(seq_len, 3, HEADS, HEAD_DIM)
    cosine, sine_table = angle_tables(seq_len)
    queries = low(rotate(proj[:, 0], cosine, sine_table))
    key_rows = low(rotate(proj[:, 1], cosine, sine_table))
    values = low(proj[:, 2])
    att = low(low_back(attention(queries, key_rows, values, block_len))).reshape(seq_len, D)
    branch = low_back(jnp.dot(att, out_weight, precision=highest))
    hidden1 = residual + branch + out_bias
    act2 = low(layer_norm(hidden1, second_gain, second_shift))
    upper = low_back(jnp.dot(act2, up_weight, precision=highest) + up_bias)
    gelu_out = low(jax.nn.gelu(upper, approximate=True))
    down = low_back(jnp.dot(gelu_out, down_weight, precision=highest))
    return hidden1 + down + down_bias

def reference(tokens, block_size, ln1_gain, ln1_shift, qkv_weight, qkv_bias, out_weight, out_bias, ln2_gain, ln2_shift, up_weight, up_bias, down_weight, down_bias, cotangent):
    params = tuple((item.astype(jnp.float32) for item in (ln1_gain, ln1_shift, qkv_weight, qkv_bias, out_weight, out_bias, ln2_gain, ln2_shift, up_weight, up_bias, down_weight, down_bias)))
    sequences = tokens.astype(jnp.float32).reshape(SEQUENCES, SEQ, D)
    cotangents = cotangent.astype(jnp.float32).reshape(SEQUENCES, SEQ, D)

    def one_sequence(totals, item):
        residual, seq_cot, block_len = item
        result, pull = jax.vjp(lambda first, second: forward(first, second, block_len), residual, params)
        grad_in, grad_params = pull(seq_cot)
        totals = jax.tree.map(lambda left, right: left + right, totals, grad_params)
        return (totals, (result, grad_in))
    zeros = jax.tree.map(jnp.zeros_like, params)
    totals, (results, grads_in) = lax.scan(one_sequence, zeros, (sequences, cotangents, block_size))
    return (results.reshape(TOKENS, D).astype(jnp.bfloat16), grads_in.reshape(TOKENS, D).astype(jnp.bfloat16), totals[0], totals[1], totals[2], totals[3], totals[4], totals[5], totals[6], totals[7], totals[8], totals[9], totals[10], totals[11])
```

```python
import itertools

import jax
import jax.numpy as jnp
import numpy as np
from jax import lax
from jax.experimental import pallas as pl
from jax.experimental.pallas import tpu as pltpu
from jax.sharding import PartitionSpec as P

HEAD_DIM = 64
MESH = pl.DeviceIdType.MESH
F32 = jnp.float32
BF16 = jnp.bfloat16
NEG = -1e30
EPS = 1e-05
T = 128
C = 256
GEO = (("q", 3, 48), ("o", 1, 48), ("u", 1, 192), ("d", 1, 192))


def mm(a, b):
    return lax.dot_general(a, b, (((1,), (0,)), ((), ())), preferred_element_type=F32)


def mm_nt(a, b):
    return lax.dot_general(a, b, (((1,), (1,)), ((), ())), preferred_element_type=F32)


def mm_tn(a, b):
    return lax.dot_general(a, b, (((0,), (0,)), ((), ())), preferred_element_type=F32)


def norm_stats(v):
    mean = jnp.mean(v, axis=-1, keepdims=True)
    cen = v - mean
    inv = lax.rsqrt(jnp.mean(cen * cen, axis=-1, keepdims=True) + EPS)
    return cen * inv, inv


def norm_back(grad, normed, inv, gain):
    g = grad * gain
    return inv * (
        g
        - jnp.mean(g, axis=-1, keepdims=True)
        - normed * jnp.mean(g * normed, axis=-1, keepdims=True)
    )


def swap_halves(v):
    lane = lax.broadcasted_iota(jnp.int32, v.shape, 1)
    low = lax.rem(lane, 64) < 32
    return jnp.where(low, pltpu.roll(v, 96, 1), pltpu.roll(v, 32, 1))


def tables(half_len):
    freqs = np.exp(
        np.arange(HEAD_DIM // 2, dtype=np.float32)
        * np.float32(-2.0 * np.log(10000.0) / HEAD_DIM)
    ).astype(np.float32)
    angles = np.arange(half_len, dtype=np.float32)[:, None] * freqs[None, :]
    angles = angles.astype(np.float32)
    cos, sin = np.cos(angles), np.sin(angles)
    return (
        np.concatenate([cos, cos, cos, cos], 1).astype(np.float32),
        np.concatenate([-sin, sin, -sin, sin], 1).astype(np.float32),
    )


def layer_kernel(
    cos_ref, sin_ref, lnp_ref, bs_ref, bias_ref,
    tok_ref, cot_ref, in_q, in_o, in_u, in_d,
    act_out, tgrad_out, small_out, fin_q, fin_o, fin_u, fin_d,
    x, a1, qs, ks, vs, att, lse, hid, a2, gelu, gp, cot,
    w_q, w_o, w_u, w_d, g_q,
    biases, bs_buf, m_same, m_lt, m_le,
    e1s, e1r, e2s, e2r, ybuf, hals, halr, halz, tg, dk, dv,
    ra_q, rb_q, rc_q, rd_q, ra_o, rb_o, rc_o, rd_o, ra_u, rb_u, rc_u, rd_u, ra_d, rb_d, rc_d, rd_d,
    sm, smr, ub, qb,
    ss, rs, ls,
):
    R = tok_ref.shape[0]
    D = tok_ref.shape[1]
    w = lax.axis_index("wide")
    z = lax.axis_index("narrow")
    c = lax.rem(w, 2)
    xx = lax.rem(lax.div(w, 2), 2)
    yy = lax.rem(lax.div(w, 4), 2)
    t = lax.div(z, 2)
    h = lax.rem(z, 2)
    wc = w + 1 - 2 * c
    wx = w + 2 - 4 * xx
    wy = w + 4 - 8 * yy
    wd = wx + 4 - 8 * yy
    z1 = z + 1 - 2 * h
    z2 = z + 2 - 4 * t
    z3 = 3 - z
    entry = 2 - c
    far = 3 - 3 * c
    home = c == t
    is_entry = z == entry
    is_far = z == far

    sends, recvs, locals_ = itertools.count(), itertools.count(), itertools.count()
    pending = []

    def take(counter, n=1):
        first = next(counter)
        for _ in range(n - 1):
            next(counter)
        return first

    def when(cond, fn):
        if cond is None:
            fn()
        else:
            @pl.when(cond)
            def _():
                fn()

    def remote(src, dst, si, ri, dev):
        return pltpu.make_async_remote_copy(
            src_ref=src, dst_ref=dst, send_sem=ss.at[si], recv_sem=rs.at[ri],
            device_id=dev, device_id_type=MESH,
        )

    def send(src, dst, ri, dev, cond=None, group=pending):
        cp = remote(src, dst, take(sends), ri, dev)
        when(cond, lambda: cp.start())
        group.append((cond, lambda: cp.wait_send()))

    def sent(group):
        for cond, wait in group:
            when(cond, wait)

    def recv(dst, ri, cond=None):
        cp = remote(dst, dst, 0, ri, (wc, z))
        when(cond, lambda: cp.wait_recv())

    def local(src, dst, cond=None):
        cp = pltpu.make_async_copy(src, dst, ls.at[take(locals_)])
        when(cond, lambda: cp.start())
        return lambda: when(cond, lambda: cp.wait())

    def rows(start, n):
        return pl.ds(pl.multiple_of(start, 128), n)

    W = {"q": w_q, "o": w_o, "u": w_u, "d": w_d}
    IN = {"q": in_q, "o": in_o, "u": in_u, "d": in_d}
    FIN = {"q": fin_q, "o": fin_o, "u": fin_u, "d": fin_d}
    G = {"q": g_q, "o": w_o, "u": w_u, "d": w_d}
    RA = {"q": ra_q, "o": ra_o, "u": ra_u, "d": ra_d}
    RB = {"q": rb_q, "o": rb_o, "u": rb_u, "d": rb_d}
    RC = {"q": rc_q, "o": rc_o, "u": rc_u, "d": rc_d}
    RD = {"q": rd_q, "o": rd_o, "u": rd_u, "d": rd_d}

    barrier = pltpu.get_barrier_semaphore()
    partners = [
        (wc, z), (wx, z), (wy, z), (wd, z), (w, z1), (w, z2), (w, z3), (wc, z2), (wc, z3),
    ]
    for dev in partners:
        pl.semaphore_signal(barrier, inc=1, device_id=dev, device_id_type=MESH)
    pl.semaphore_wait(barrier, len(partners))

    bs_r = take(recvs)
    send(bs_ref, bs_buf, bs_r, (wc, z))

    halves = [pl.ds(k * (R // 2), R // 2) for k in range(2)]

    def block(ref, b, k):
        return ref.at[pl.ds(pl.multiple_of(R * b + k * (R // 2), 128), R // 2)]

    tok_r = take(recvs, 6)
    tok_local = local(tok_ref, x.at[pl.ds(pl.multiple_of(R * c, 128), R)], home)
    first_c = 1 - c
    slot = first_c * (4 - z)
    zt = first_c + c * (z + 2)
    for k in range(2):
        src = tok_ref.at[halves[k]]
        send(src, block(x, c, k), tok_r + 2 * c + k, (wc, z), home)
        send(src, block(x, slot, k), tok_r + 2 * slot + k, (wc, zt), jnp.logical_not(home))
    zero_halo = h == 0

    @pl.when(zero_halo)
    def _():
        x[pl.ds(2 * R, R), :] = jnp.zeros((R, D), BF16)

    w_native = {}
    w_sent = {g: [] for g, _, _ in GEO}
    wz_r = {g: take(recvs, 2) for g, _, _ in GEO}
    wxy_r = {g: take(recvs, 6) for g, _, _ in GEO}

    def weights_out(g):
        src = IN[g].at[:, yy, xx]
        dst = W[g].at[:, h, yy, xx]
        send(src, dst, wz_r[g] + h, (w, entry), home)
        send(src, dst, wz_r[g] + h, (w, z1), home)

    def weights_native(g):
        w_native[g] = local(IN[g], W[g].at[:, h], home)

    def weights_spread(g):
        for s in range(2):
            foreign = jnp.logical_not(jnp.logical_and(home, h == s))
            piece = W[g].at[:, s, yy, xx]
            recv(piece, wz_r[g] + s, foreign)
            send(piece, piece, wz_r[g] + s, (w, far), is_entry, w_sent[g])
            for j, dev in enumerate((wx, wy, wd)):
                send(piece, piece, wxy_r[g] + 3 * s + j, (dev, z), foreign, w_sent[g])

    def weights_wait(g):
        w_native[g]()
        for s in range(2):
            foreign = jnp.logical_not(jnp.logical_and(home, h == s))
            for j, (py, px) in enumerate(((yy, 1 - xx), (1 - yy, xx), (1 - yy, 1 - xx))):
                recv(W[g].at[:, s, py, px], wxy_r[g] + 3 * s + j, foreign)

    bias_r = take(recvs, 2)
    bias_local = local(bias_ref, biases.at[h], home)
    for dz in (entry, z1, far):
        send(bias_ref, biases.at[h], bias_r + h, (w, dz), home)
    weights_out("q")
    for g in ("q", "o", "u", "d"):
        weights_native(g)
    halo_src = jnp.logical_and(c == 1, z == 2)
    for k in range(2):
        send(tok_ref.at[halves[k]], block(x, 2, k), tok_r + 4 + k, (w, 3), halo_src)

    lnp = lnp_ref
    gain1, shift1 = lnp[0:1, :], lnp[1:2, :]

    def norm_block(b):
        def step(i, _):
            r = rows(R * b + i * C, C)
            normed, _inv = norm_stats(x[r, :].astype(F32))
            a1[r, :] = (normed * gain1 + shift1).astype(BF16)
            return 0

        lax.fori_loop(0, R // C, step, 0)

    recv(bs_buf, bs_r)
    pick = (t == c).astype(jnp.int32)
    bl = bs_ref[0:1, :] * pick + bs_buf[0:1, :] * (1 - pick)
    bl = jnp.concatenate([bl, bl], axis=1)

    def block_of(v):
        return jnp.where(
            bl == 4,
            lax.shift_right_logical(v, 2),
            jnp.where(bl == 8, lax.shift_right_logical(v, 3), lax.shift_right_logical(v, 4)),
        )

    key_no = block_of(lax.broadcasted_iota(jnp.int32, (T, 2 * T), 0))
    row_no = block_of(lax.rem(lax.broadcasted_iota(jnp.int32, (T, 2 * T), 1), T))
    m_same[...] = jnp.where(key_no == row_no, 0.0, NEG)
    m_lt[...] = jnp.where(key_no < row_no, 0.0, NEG)
    m_le[...] = jnp.where(key_no <= row_no, 0.0, NEG)

    takes_halo = jnp.logical_and(c == 1, h == 1)
    feeds = jnp.logical_and(c == 1, z == 1)
    away = jnp.logical_not(home)
    tok_local()
    for k in range(2):
        recv(block(x, 2, k), tok_r + 4 + k, takes_halo)
        send(block(x, 2, k), block(x, 1, k), tok_r + 2 + k, (w, 0), feeds)
        send(block(x, 2, k), block(x, 2, k), tok_r + 4 + k, (wc, z), takes_halo)
    for k in range(2):
        recv(block(x, c, k), tok_r + 2 * c + k, away)
        send(block(x, c, k), block(x, c, k), tok_r + 2 * c + k, (wc, z), away)
    weights_spread("q")
    for g in ("o", "u", "d"):
        weights_out(g)
    cot_r = take(recvs, 4)
    cot_local = local(cot_ref, cot.at[pl.ds(pl.multiple_of(R * c, 128), R)], home)
    for k in range(2):
        src = cot_ref.at[halves[k]]
        send(src, block(cot, c, k), cot_r + 2 * c + k, (wc, z), home)
        send(src, block(cot, 1 - c, k), cot_r + 2 * (1 - c) + k, (wc, z2), away)
    for k in range(2):
        recv(block(x, 1 - c, k), tok_r + 2 * (1 - c) + k)
    for k in range(2):
        recv(block(x, 2, k), tok_r + 4 + k, jnp.logical_and(c == 0, h == 1))
    norm_block(0)
    norm_block(1)
    norm_block(2)

    bias_local()
    recv(biases.at[0], bias_r, jnp.logical_not(jnp.logical_and(home, h == 0)))
    recv(biases.at[1], bias_r + 1, jnp.logical_not(jnp.logical_and(home, h == 1)))
    bias_rows = (biases[0] + biases[1]).astype(F32)
    weights_wait("q")
    HC = 6 * HEAD_DIM
    NP = HC // 128

    def wq(j):
        return w_q[j].reshape(HC, D)

    def cos_sin(place, n):
        r = rows(place, n)
        return cos_ref[r, :], sin_ref[r, :]

    def project(i, halo):
        r = rows(i * C, C)
        a = a1[r, :]
        place = (i * C - 2 * R) if halo else (R * h + lax.rem(i * C, R))
        cs, sn = cos_sin(place, C)
        if not halo:
            qv = mm_nt(a, wq(0)) + bias_rows[0:1, :HC]
            for p in range(NP):
                v = qv[:, p * 128 : p * 128 + 128]
                qs[p, r, :] = ((v * cs + swap_halves(v) * sn) * 0.125).astype(BF16)
        kv = mm_nt(a, wq(1)) + bias_rows[1:2, :HC]
        for p in range(NP):
            v = kv[:, p * 128 : p * 128 + 128]
            ks[p, r, :] = (v * cs + swap_halves(v) * sn).astype(BF16)
        vv = mm_nt(a, wq(2)) + bias_rows[2:3, :HC]
        for p in range(NP):
            vs[p, r, :] = vv[:, p * 128 : p * 128 + 128].astype(BF16)

    def loop(lo, hi, fn):
        def step(i, _):
            fn(i)
            return 0

        lax.fori_loop(lo, hi, step, 0)

    loop(0, 2 * R // C, lambda i: project(i, False))
    loop(2 * R // C, 3 * R // C, lambda i: project(i, True))
    weights_spread("o")
    weights_spread("u")

    halo_bias = jnp.where(h == 1, 0.0, NEG).astype(F32)
    lane = lax.broadcasted_iota(jnp.int32, (1, 128), 1)
    lo_f = (lane < 64).astype(F32)
    lo_mask = lo_f.astype(BF16)
    hi_mask = (1.0 - lo_f).astype(BF16)

    def both_heads(v):
        return jnp.concatenate([v * lo_mask, v * hi_mask], axis=0)

    def one_of_each(v):
        return v[:T] * lo_f + v[T:] * (1.0 - lo_f)

    def key_parts(b, i):
        parts = []
        if b == 0:
            parts.append((T * i, T, m_same))
        if i > 0:
            parts.append((R, T * i, None))
        parts.append((R + T * i, T, m_lt if b == 0 else m_le))
        parts.append((2 * R, R, halo_bias))
        return parts

    def scores_of(p, part, qm):
        start, n, mask = part
        sc = mm_nt(ks[p, pl.ds(start, n), :], qm)
        if mask is None:
            return sc
        if mask is halo_bias:
            return sc + halo_bias
        return sc + mask[...]

    chunks = [(b, i) for b in range(2) for i in range(R // T)]

    def attend(p):
        for n, (b, i) in enumerate(chunks):
            r = pl.ds(R * b + T * i, T)
            qm = both_heads(qs[p, r, :])
            parts = key_parts(b, i)
            sc = [scores_of(p, part, qm) for part in parts]
            top = None
            for v in sc:
                m = jnp.max(v, axis=0, keepdims=True)
                top = m if top is None else jnp.maximum(top, m)
            total, out = None, None
            for part, v in zip(parts, sc):
                e = jnp.exp(v - top)
                l = jnp.sum(e, axis=0, keepdims=True)
                o = mm_tn(vs[p, pl.ds(part[0], part[1]), :], e.astype(BF16))
                total = l if total is None else total + l
                out = o if out is None else out + o
            out = out / total
            att[p, r, :] = one_of_each(out.T).astype(BF16)
            lse[p, n] = top + jnp.log(total)

    loop(0, NP, attend)
    weights_spread("d")

    e1_r = take(recvs, 4)
    e1_s = take(sends, 4)
    NC = 2 * R // C
    weights_wait("o")

    def swap_out(i, si, ri):
        r = rows(i * C, C)
        remote(e1s.at[r], e1r.at[r], si + i, ri + i, (wc, z)).start()

    def swap_in(i, ri):
        r = rows(i * C, C)
        remote(e1r.at[r], e1r.at[r], 0, ri + i, (wc, z)).wait_recv()

    def swap_done(i, si):
        r = rows(i * C, C)
        remote(e1s.at[r], e1r.at[r], si + i, 0, (wc, z)).wait_send()

    def pairs(ref, r):
        return jnp.concatenate([ref[p, r, :] for p in range(NP)], axis=1)

    def out_project(i):
        r = rows(i * C, C)
        e1s[r, :] = mm(pairs(att, r), w_o[0].reshape(HC, D)).astype(BF16)
        swap_out(i, e1_s, e1_r)

    loop(0, NC, out_project)
    cot_local()
    for k in range(2):
        recv(block(cot, c, k), cot_r + 2 * c + k, away)
        send(block(cot, c, k), block(cot, c, k), cot_r + 2 * c + k, (wc, z), away)
    for k in range(2):
        recv(block(cot, 1 - c, k), cot_r + 2 * (1 - c) + k)
    weights_wait("u")
    weights_wait("d")

    sm[...] = jnp.zeros(sm.shape, F32)
    ub[...] = jnp.zeros(ub.shape, F32)
    qb[...] = jnp.zeros(qb.shape, F32)
    out_bias, gain2, shift2, down_bias = lnp[2:3, :], lnp[3:4, :], lnp[4:5, :], lnp[5:6, :]
    KG = float(np.sqrt(2.0 / np.pi))

    def feed(i):
        r = rows(i * C, C)
        swap_in(i, e1_r)
        hv = x[r, :].astype(F32) + e1s[r, :].astype(F32) + e1r[r, :].astype(F32) + out_bias
        hid[r, :] = hv
        normed, _inv = norm_stats(hv)
        act = (normed * gain2 + shift2).astype(BF16)
        a2[r, :] = act
        cv = cot[r, :]
        for s in range(2):
            cols = pl.ds(s * D, D)
            u = mm(act, w_u[0, s].reshape(D, D)) + bias_rows[3:4, s * D : (s + 1) * D]
            u2 = u * u
            th = jnp.tanh(KG * u * (1.0 + 0.044715 * u2))
            half = 0.5 * (1.0 + th)
            gelu[r, cols] = (u * half).astype(BF16)
            slope = half + 0.5 * u * (1.0 - th * th) * (KG * (1.0 + 3 * 0.044715 * u2))
            gg = mm_nt(cv, w_d[0, s].reshape(D, D))
            gu = (gg * slope).astype(BF16)
            gp[r, cols] = gu
            ub[0:1, cols] += jnp.sum(gu.astype(F32), axis=0, keepdims=True)

    loop(0, NC, feed)
    loop(0, NC, lambda i: swap_done(i, e1_s))

    e2_r, e2_s = take(recvs, 2), take(sends, 2)
    HB = R // C

    def down_of(r):
        return mm(gelu[r, 0:D], w_d[0, 0].reshape(D, D)) + mm(gelu[r, D : 2 * D], w_d[0, 1].reshape(D, D))

    def down_other(i):
        r = rows(R * (1 - c) + i * C, C)
        d = rows(i * C, C)
        e2s[d, :] = down_of(r).astype(BF16)
        remote(e2s.at[d], e2r.at[d], e2_s + i, e2_r + i, (wc, z)).start()

    loop(0, HB, down_other)

    e3_r, e3_s = take(recvs, 4), take(sends, 4)

    def back_up(i):
        r = rows(i * C, C)
        e1s[r, :] = (
            mm_nt(gp[r, 0:D], w_u[0, 0].reshape(D, D)) + mm_nt(gp[r, D : 2 * D], w_u[0, 1].reshape(D, D))
        ).astype(BF16)
        d = rows(i * C, C)

    loop(0, NC, back_up)

    def down_own(i):
        r = rows(R * c + i * C, C)
        d = rows(i * C, C)
        part = down_of(r)
        remote(e2r.at[d], e2r.at[d], 0, e2_r + i, (wc, z)).wait_recv()
        y = hid[r, :] + part + e2r[d, :].astype(F32) + down_bias
        ybuf[d, :] = y.astype(BF16)
        sm[5:6, :] += jnp.sum(cot[r, :].astype(F32), axis=0, keepdims=True)

    loop(0, HB, down_own)
    loop(0, NC, lambda i: swap_out(i, e3_s, e3_r))
    z_orig = 2 * c + h
    y_r = take(recvs)
    y_local = local(ybuf, act_out, home)
    send(ybuf, act_out, y_r, (wc, z_orig), away)

    ra_r = {g: take(recvs, 2) for g, _, _ in GEO}
    rb_r = {g: take(recvs, 2) for g, _, _ in GEO}
    rc_r = {g: take(recvs, 2) for g, _, _ in GEO}
    rd_r = {g: take(recvs, 2) for g, _, _ in GEO}
    fin_r = {g: take(recvs, 4) for g, _, _ in GEO}
    fin_local = {}
    size = {g: (n, r) for g, n, r in GEO}

    def add(dst, src):
        dst[...] = (dst[...].astype(F32) + src[...].astype(F32)).astype(BF16)

    def reduce_a(g):
        send(G[g].at[:, 0, :, 1 - xx], RA[g].at[0], ra_r[g], (wx, z))
        send(G[g].at[:, 1, 1 - yy, :], RA[g].at[1], ra_r[g] + 1, (wy, z))

    def reduce_b(g):
        n, r = size[g]
        recv(RA[g].at[0], ra_r[g])
        for k in range(n):
            for m in range(2):
                add(G[g].at[k, 0, m, xx], RA[g].at[0, k, m])
        send(G[g].at[:, 0, 1 - yy, xx], RB[g].at[0], rb_r[g], (wy, z))
        recv(RA[g].at[1], ra_r[g] + 1)
        for k in range(n):
            for m in range(2):
                add(G[g].at[k, 1, yy, m], RA[g].at[1, k, m])
        send(G[g].at[:, 1, yy, 1 - xx], RB[g].at[1], rb_r[g] + 1, (wx, z))

    def reduce_c(g):
        n, r = size[g]
        for s in range(2):
            recv(RB[g].at[s], rb_r[g] + s)
            for k in range(n):
                add(G[g].at[k, s, yy, xx], RB[g].at[s, k])
            piece = G[g].at[:, s, yy, xx]
            send(piece, RC[g].at[s], rc_r[g] + s, (w, entry), is_far)
            send(piece, RD[g].at[0], rd_r[g], (w, z1), jnp.logical_and(home, h == 1 - s))

    def reduce_d(g):
        n, r = size[g]
        for s in range(2):
            recv(RC[g].at[s], rc_r[g] + s, is_entry)

            @pl.when(is_entry)
            def _():
                for k in range(n):
                    add(G[g].at[k, s, yy, xx], RC[g].at[s, k])

            send(G[g].at[:, s, yy, xx], RD[g].at[1], rd_r[g] + 1, (w, 2 * c + s), is_entry)

    def reduce_e(g):
        n, r = size[g]
        recv(RD[g].at[0], rd_r[g], home)
        recv(RD[g].at[1], rd_r[g] + 1, home)

        @pl.when(home)
        def _():
            for k in range(n):
                dst = G[g].at[k, h, yy, xx]
                dst[...] = (
                    dst[...].astype(F32) + RD[g][0, k].astype(F32) + RD[g][1, k].astype(F32)
                ).astype(BF16)

        piece = G[g].at[:, h, yy, xx]
        out = FIN[g].at[:, yy, xx]
        fin_local[g] = local(piece, out, home)
        for j, dev in enumerate((wx, wy, wd)):
            send(piece, out, fin_r[g] + j, (dev, z), home)
        send(piece, out, fin_r[g] + 3, (wc, z), home)

    def reduce_f(g):
        for j, (py, px) in enumerate(((yy, 1 - xx), (1 - yy, xx), (1 - yy, 1 - xx))):
            piece = FIN[g].at[:, py, px]
            recv(piece, fin_r[g] + j, home)
            send(piece, piece, fin_r[g] + j, (wc, z), home)

    def reduce_g(g):
        fin_local[g]()
        for j, (py, px) in enumerate(
            ((yy, 1 - xx), (1 - yy, xx), (1 - yy, 1 - xx), (yy, xx))
        ):
            recv(FIN[g].at[:, py, px], fin_r[g] + j, away)

    def grad_down(j):
        cols = pl.ds(pl.multiple_of(j * 384, 128), 384)
        g = mm_tn(gelu[:, cols], cot[...])
        w_d[0, lax.div(j, 2), lax.rem(j, 2)] = g.astype(BF16).reshape(2, 192, D)

    def grad_up(j):
        s, half = lax.div(j, 2), lax.rem(j, 2)
        g = mm_tn(
            a2[:, pl.ds(pl.multiple_of(half * 384, 128), 384)],
            gp[:, pl.ds(pl.multiple_of(s * D, 128), D)],
        )
        w_u[0, s, half] = g.astype(BF16).reshape(2, 192, D)

    sent(w_sent["d"])
    loop(0, 4, grad_down)
    reduce_a("d")
    sent(w_sent["u"])
    loop(0, 4, grad_up)
    reduce_a("u")

    def norm2_back(i):
        r = rows(i * C, C)
        swap_in(i, e3_r)
        g2 = e1s[r, :].astype(F32) + e1r[r, :].astype(F32)
        normed, inv = norm_stats(hid[r, :])
        gh = cot[r, :].astype(F32) + norm_back(g2, normed, inv, gain2)
        hid[r, :] = gh
        own = (lax.div(i, HB) == c).astype(F32)
        sm[3:4, :] += own * jnp.sum(g2 * normed, axis=0, keepdims=True)
        sm[4:5, :] += own * jnp.sum(g2, axis=0, keepdims=True)
        sm[2:3, :] += own * jnp.sum(gh, axis=0, keepdims=True)

    loop(0, NC, norm2_back)
    loop(0, NC, lambda i: swap_done(i, e3_s))

    def grad_att(i):
        r = rows(i * C, C)
        br = hid[r, :].astype(BF16)
        e1s[r, :] = br
        ga = mm_nt(br, w_o[0].reshape(HC, D)).astype(BF16)
        for p in range(NP):
            a2[r, p * 128 : p * 128 + 128] = ga[:, p * 128 : p * 128 + 128]

    loop(0, NC, grad_att)
    everything = pl.ds(0, 2 * R)
    sent(w_sent["o"])
    g_out = mm_tn(pairs(att, everything), e1s[...])
    w_o[0] = g_out.astype(BF16).reshape(2, 2, 2, 48, D)
    reduce_a("o")
    reduce_b("d")

    def attend_back(p):
        dk[...] = jnp.zeros(dk.shape, F32)
        dv[...] = jnp.zeros(dv.shape, F32)
        cols = pl.ds(pl.multiple_of(p * 128, 128), 128)
        for n, (b, i) in enumerate(chunks):
            r = pl.ds(R * b + T * i, T)
            qm = both_heads(qs[p, r, :])
            gm = both_heads(a2[r, cols])
            parts = key_parts(b, i)
            log_total = lse[p, n]
            delta, probs, gprobs = None, [], []
            for part in parts:
                pr = jnp.exp(scores_of(p, part, qm) - log_total)
                dp = mm_nt(vs[p, pl.ds(part[0], part[1]), :], gm)
                dl = jnp.sum(pr * dp, axis=0, keepdims=True)
                delta = dl if delta is None else delta + dl
                probs.append(pr)
                gprobs.append(dp)
            dq = None
            for part, pr, dp in zip(parts, probs, gprobs):
                k = pl.ds(part[0], part[1])
                ds = (pr * (dp - delta)).astype(BF16)
                dv[k, :] += mm(pr.astype(BF16), gm)
                dk[k, :] += mm(ds, qm)
                d = mm_tn(ks[p, k, :], ds)
                dq = d if dq is None else dq + d
            dq = one_of_each(dq.T) * 0.125
            cs, sn = cos_sin(R * h + T * i, T)
            dq = (dq * cs - swap_halves(dq) * sn).astype(BF16)
            qs[p, r, :] = dq
        for b in range(3):
            cs, sn = cos_sin(R * h if b < 2 else 0, R)
            r = pl.ds(R * b, R)
            v = dk[r, :]
            ks[p, r, :] = (v * cs - swap_halves(v) * sn).astype(BF16)
            vs[p, r, :] = dv[r, :].astype(BF16)

    attend_back(0)
    reduce_b("u")
    reduce_c("d")
    attend_back(1)
    reduce_b("o")
    reduce_c("u")
    reduce_d("d")
    attend_back(2)
    reduce_c("o")
    reduce_d("u")
    reduce_e("d")

    def grad_qkv(j, ref, n):
        r = pl.ds(0, n)
        lhs = pairs(ref, r)
        g_q[j] = mm_tn(lhs, a1[r, :]).astype(BF16).reshape(2, 2, 2, 48, D)
        qb[j : j + 1, :] += jnp.sum(lhs.astype(F32), axis=0, keepdims=True)

    grad_qkv(0, qs, 2 * R)
    grad_qkv(1, ks, 3 * R)
    grad_qkv(2, vs, 3 * R)
    reduce_a("q")

    def back_qkv(r, halo):
        g = mm(pairs(ks, r), wq(1)) + mm(pairs(vs, r), wq(2))
        return g if halo else g + mm(pairs(qs, r), wq(0))

    def halo_back(i):
        r = rows(2 * R + i * C, C)
        hals[rows(i * C, C), :] = back_qkv(r, True).astype(BF16)

    loop(0, HB, halo_back)
    hal_r = take(recvs)
    send(hals, halr, hal_r, (wc, z), c == 0)
    e4_r, e4_s = take(recvs, 2), take(sends, 2)
    loop(0, HB, lambda i: remote(
        e2s.at[rows(i * C, C)], e2r.at[rows(i * C, C)], e2_s + i, 0, (wc, z)).wait_send())

    def other_back(i):
        d = rows(i * C, C)
        e2s[d, :] = back_qkv(rows(R * (1 - c) + i * C, C), False).astype(BF16)
        remote(e2s.at[d], e2r.at[d], e4_s + i, e4_r + i, (wc, z)).start()

    loop(0, HB, other_back)
    recv(halr, hal_r, c == 1)
    halz_r = take(recvs)

    @pl.when(c == 1)
    def _():
        add(hals, halr)

    send(hals, halz, halz_r, (w, z1), jnp.logical_and(c == 1, h == 1))
    reduce_d("o")
    reduce_e("u")
    reduce_f("d")
    reduce_b("q")

    def own_back(i):
        d = rows(i * C, C)
        tg[d, :] = back_qkv(rows(R * c + i * C, C), False)

    loop(0, HB, own_back)
    gets = jnp.logical_and(c == 1, h == 0)
    recv(halz, halz_r, gets)

    @pl.when(jnp.logical_not(gets))
    def _():
        halz[...] = jnp.zeros(halz.shape, BF16)

    y_local()
    def norm1_back(i):
        d = rows(i * C, C)
        r = rows(R * c + i * C, C)
        remote(e2r.at[d], e2r.at[d], 0, e4_r + i, (wc, z)).wait_recv()
        g1 = tg[d, :] + e2r[d, :].astype(F32) + halz[d, :].astype(F32)
        normed, inv = norm_stats(x[r, :].astype(F32))
        out = hid[r, :] + norm_back(g1, normed, inv, gain1)
        sm[0:1, :] += jnp.sum(g1 * normed, axis=0, keepdims=True)
        sm[1:2, :] += jnp.sum(g1, axis=0, keepdims=True)
        halr[d, :] = out.astype(BF16)

    loop(0, HB, norm1_back)
    t_r = take(recvs)
    t_local = local(halr, tgrad_out, home)
    send(halr, tgrad_out, t_r, (wc, z_orig), away)
    reduce_c("q")
    reduce_e("o")
    reduce_f("u")

    cf = c.astype(F32)
    for j in range(3):
        sm[6 + j : 7 + j, 0:HC] = qb[j : j + 1, :] * (1.0 - cf)
        sm[6 + j : 7 + j, HC : 2 * HC] = qb[j : j + 1, :] * cf
    for s in range(2):
        sm[9 + s : 10 + s, :] = ub[0:1, s * D : (s + 1) * D] * (1.0 - cf)
        sm[11 + s : 12 + s, :] = ub[0:1, s * D : (s + 1) * D] * cf
    for k, dev in enumerate(((wc, z), (wx, z), (wy, z), (w, z1), (w, z2))):
        cp = remote(sm, smr.at[k], take(sends), take(recvs), dev)
        cp.start()
        cp.wait()
        sm[...] += smr[k]
        if k == 1:
            reduce_d("q")
    small_out[...] = sm[...]
    reduce_e("q")
    for g in ("o", "q"):
        reduce_f(g)
    for g in ("d", "u", "o", "q"):
        reduce_g(g)
    recv(act_out, y_r, away)
    recv(tgrad_out, t_r, away)
    t_local()
    loop(0, HB, lambda i: remote(
        e2s.at[rows(i * C, C)], e2r.at[rows(i * C, C)], e4_s + i, 0, (wc, z)).wait_send())
    sent(w_sent["q"])
    sent(pending)
    counts = (next(sends), next(recvs), next(locals_))
    assert counts[0] <= ss.shape[0] and counts[1] <= rs.shape[0] and counts[2] <= ls.shape[0], counts


def shards(
    tokens, block_size, ln1_gain, ln1_shift, qkv_weight, qkv_bias, out_weight, out_bias,
    ln2_gain, ln2_shift, up_weight, up_bias, down_weight, down_bias, cotangent, groups,
):
    R, D = tokens.shape
    z = lax.axis_index("narrow")
    h = lax.rem(z, 2)
    local_width = qkv_weight.shape[2]
    HC = 2 * local_width
    FC = 2 * up_weight.shape[1]
    cos, sin = tables(2 * R)
    lnp = jnp.stack(
        [ln1_gain, ln1_shift, out_bias, ln2_gain, ln2_shift, down_bias, down_bias, down_bias]
    ).astype(F32)
    bs = jnp.broadcast_to(block_size, (8, 128)).astype(jnp.int32)
    lane = jnp.arange(FC, dtype=jnp.int32)
    wide_qkv = jnp.concatenate([qkv_bias] * (FC // local_width), axis=1)
    wide_up = jnp.concatenate([up_bias] * (FC // up_bias.shape[0]))[None]
    in_q = (lane // local_width == h)[None]
    in_u = (lane // up_bias.shape[0] == h)[None]
    bias = jnp.concatenate(
        [
            jnp.where(in_q, wide_qkv, 0),
            jnp.where(in_u, wide_up, 0),
            jnp.zeros((12, FC), BF16),
        ],
        axis=0,
    ).astype(BF16)
    wq = jnp.transpose(qkv_weight, (1, 2, 0)).reshape(3, 2, 2, 48, D)
    wo = out_weight.reshape(1, 2, 2, 48, D)
    wu = up_weight.reshape(1, 2, 2, 192, D)
    wdn = down_weight.reshape(1, 2, 2, 192, D)
    anyspec = pl.BlockSpec(memory_space=pl.ANY)
    vspec = pl.BlockSpec(memory_space=pltpu.VMEM)
    sds = jax.ShapeDtypeStruct
    fins = [sds((n, 2, 2, r, D), BF16) for _, n, r in GEO]
    V = pltpu.VMEM
    weights = [V((n, 2, 2, 2, r, D), BF16) for _, n, r in GEO]
    recvs = []
    for _, n, r in GEO:
        recvs += [
            V((2, n, 2, r, D), BF16),
            V((2, n, r, D), BF16),
            V((2, n, r, D), BF16),
            V((2, n, r, D), BF16),
        ]
    NP = HC // 128
    outs = pl.pallas_call(
        layer_kernel,
        out_shape=[sds((R, D), BF16), sds((R, D), BF16), sds((16, D), F32)] + fins,
        in_specs=[vspec] * 4 + [anyspec] * 7,
        out_specs=[anyspec, anyspec, vspec] + [anyspec] * 4,
        scratch_shapes=[
            V((3 * R, D), BF16),
            V((3 * R, D), BF16),
            V((NP, 2 * R, 128), BF16),
            V((NP, 3 * R, 128), BF16),
            V((NP, 3 * R, 128), BF16),
            V((NP, 2 * R, 128), BF16),
            V((NP, 2 * R // T, 1, 2 * T), F32),
            V((2 * R, D), F32),
            V((2 * R, D), BF16),
            V((2 * R, FC), BF16),
            V((2 * R, FC), BF16),
            V((2 * R, D), BF16),
            *weights,
            V((3, 2, 2, 2, 48, D), BF16),
            V((2, 16, FC), BF16),
            V((8, 128), jnp.int32),
            V((T, 2 * T), F32),
            V((T, 2 * T), F32),
            V((T, 2 * T), F32),
            V((2 * R, D), BF16),
            V((2 * R, D), BF16),
            V((R, D), BF16),
            V((R, D), BF16),
            V((R, D), BF16),
            V((R, D), BF16),
            V((R, D), BF16),
            V((R, D), BF16),
            V((R, D), F32),
            V((3 * R, 128), F32),
            V((3 * R, 128), F32),
            *recvs,
            V((16, D), F32),
            V((5, 16, D), F32),
            V((8, FC), F32),
            V((8, HC), F32),
            pltpu.SemaphoreType.DMA((200,)),
            pltpu.SemaphoreType.DMA((140,)),
            pltpu.SemaphoreType.DMA((24,)),
        ],
        compiler_params=pltpu.CompilerParams(
            collective_id=0, has_side_effects=True, vmem_limit_bytes=62 * 1024 * 1024
        ),
        name="layer",
    )(jnp.asarray(cos), jnp.asarray(sin), lnp, bs, bias, tokens, cotangent, wq, wo, wu, wdn)
    act, tgrad, small, fq, fo, fu, fd = outs
    grads = [
        jnp.transpose(fq.reshape(3, local_width, D), (2, 0, 1)).astype(F32),
        fo.reshape(local_width, D).astype(F32),
        fu.reshape(D, D).astype(F32),
        fd.reshape(D, D).astype(F32),
    ]
    if groups > 1:
        ids = [[g * 8 + k for g in range(groups)] for k in range(8)]
        grads, small = lax.psum((grads, small), "wide", axis_index_groups=ids)
    gq, go, gu, gd = grads
    qb = lax.dynamic_slice_in_dim(small[6:9], local_width * z, local_width, axis=1)
    ubias = lax.dynamic_slice_in_dim(small[9:13], z, 1, axis=0)[0]
    return (
        act, tgrad, small[0], small[1], gq, qb, go, small[2], small[3], small[4], gu, ubias, gd, small[5],
    )


def solution(mesh):
    both = P(("wide", "narrow"), None)
    in_specs = (
        both, P("wide"), P(), P(), P(None, None, "narrow"), P(None, "narrow"), P("narrow", None), P(),
        P(), P(), P(None, "narrow"), P("narrow"), P("narrow", None), P(), both,
    )
    out_specs = (
        both, both, P(), P(), P(None, None, "narrow"), P(None, "narrow"), P("narrow", None), P(),
        P(), P(), P(None, "narrow"), P("narrow"), P("narrow", None), P(),
    )
    groups = mesh.shape["wide"] // 8

    def body(*args):
        return shards(*args, groups)

    return jax.shard_map(body, mesh=mesh, in_specs=in_specs, out_specs=out_specs, check_vma=False)
```

```python
import itertools

import jax
import jax.numpy as jnp
import numpy as np
from jax import lax
from jax.experimental import pallas as pl
from jax.experimental.pallas import tpu as pltpu
from jax.sharding import PartitionSpec as P

HEAD_DIM = 64
MESH = pl.DeviceIdType.MESH
F32 = jnp.float32
BF16 = jnp.bfloat16
NEG = -1e30
EPS = 1e-05
T = 128
C = 256
Q, O, U0, U1, D0, D1, Q0, Q1, Q2 = range(9)
GEO = ((Q, 9, 16), (O, 3, 16), (U0, 1, 96), (U1, 1, 96), (D0, 1, 96), (D1, 1, 96))
RED = (
    (D0, 1, 96), (D1, 1, 96), (U0, 1, 96), (U1, 1, 96),
    (O, 3, 16), (Q0, 3, 16), (Q1, 3, 16), (Q2, 3, 16),
)
DIRECT = (O, Q0, Q1, Q2)


def mm(a, b):
    return lax.dot_general(a, b, (((1,), (0,)), ((), ())), preferred_element_type=F32)


def mm_nt(a, b):
    return lax.dot_general(a, b, (((1,), (1,)), ((), ())), preferred_element_type=F32)


def mm_tn(a, b):
    return lax.dot_general(a, b, (((0,), (0,)), ((), ())), preferred_element_type=F32)


def norm_stats(v):
    mean = jnp.mean(v, axis=-1, keepdims=True)
    cen = v - mean
    inv = lax.rsqrt(jnp.mean(cen * cen, axis=-1, keepdims=True) + EPS)
    return cen * inv, inv


def norm_back(grad, normed, inv, gain):
    g = grad * gain
    return inv * (
        g
        - jnp.mean(g, axis=-1, keepdims=True)
        - normed * jnp.mean(g * normed, axis=-1, keepdims=True)
    )


def swap_halves(v):
    lane = lax.broadcasted_iota(jnp.int32, v.shape, 1)
    low = lax.rem(lane, 64) < 32
    return jnp.where(low, pltpu.roll(v, 96, 1), pltpu.roll(v, 32, 1))


def tables(half_len):
    freqs = np.exp(
        np.arange(HEAD_DIM // 2, dtype=np.float32)
        * np.float32(-2.0 * np.log(10000.0) / HEAD_DIM)
    ).astype(np.float32)
    angles = np.arange(half_len, dtype=np.float32)[:, None] * freqs[None, :]
    angles = angles.astype(np.float32)
    cos, sin = np.cos(angles), np.sin(angles)
    return (
        np.concatenate([cos, cos, cos, cos], 1).astype(np.float32),
        np.concatenate([-sin, sin, -sin, sin], 1).astype(np.float32),
    )


def layer_kernel(
    cos_ref, sin_ref, g1_ref, s1_ref, ob_ref, g2_ref, s2_ref, db_ref, upb_ref, qkvb_ref, bs_ref,
    tok_ref, cot_ref, in_q, in_o, in_u, in_d,
    act_out, tgrad_out, small_out, fin_q, fin_o, fin_u, fin_d,
    x, a1, qs, ks, vs, att, lse, hid, a2, gelu, gp, cot,
    w_q, w_o, w_u, w_d, g_q, g_d,
    bias_own, biases, bs_own, bs_buf, m_same, m_lt, m_le,
    e1s, e1r, e2s, e2r, e3r, e4r, ybuf, hals, halr, halz, tg, dk, dv,
    *rest,
):
    sm, smr, smz, ub, qb, ss, rs, ls = rest[-8:]
    RA, RB, RC, RD = ({g: rest[4 * k + i] for k, (g, _, _) in enumerate(RED)} for i in range(4))
    R = tok_ref.shape[0]
    D = tok_ref.shape[1]
    w = lax.axis_index("wide")
    z = lax.axis_index("narrow")
    c = lax.rem(w, 2)
    xx = lax.rem(lax.div(w, 2), 2)
    yy = lax.rem(lax.div(w, 4), 2)
    t = lax.div(z, 2)
    h = lax.rem(z, 2)
    wc = w + 1 - 2 * c
    wx = w + 2 - 4 * xx
    wy = w + 4 - 8 * yy
    z1 = z + 1 - 2 * h
    z2 = z + 2 - 4 * t
    z3 = 3 - z
    entry = 2 - c
    far = 3 - 3 * c
    home = c == t
    away = jnp.logical_not(home)
    is_entry = z == entry
    is_far = z == far

    sends, recvs, locals_ = itertools.count(), itertools.count(), itertools.count()
    pending = []

    def take(counter, n=1):
        first = next(counter)
        for _ in range(n - 1):
            next(counter)
        return first

    def when(cond, fn):
        if cond is None:
            fn()
        else:
            @pl.when(cond)
            def _():
                fn()

    def remote(src, dst, si, ri, dev):
        return pltpu.make_async_remote_copy(
            src_ref=src, dst_ref=dst, send_sem=ss.at[si], recv_sem=rs.at[ri],
            device_id=dev, device_id_type=MESH,
        )

    def send(src, dst, ri, dev, cond=None, group=pending):
        cp = remote(src, dst, take(sends), ri, dev)
        when(cond, lambda: cp.start())
        group.append((cond, lambda: cp.wait_send()))

    def sent(group):
        for cond, wait in group:
            when(cond, wait)
        group.clear()

    def recv(dst, ri, cond=None):
        cp = remote(dst, dst, 0, ri, (wc, z))
        when(cond, lambda: cp.wait_recv())

    def local(src, dst, cond=None):
        cp = pltpu.make_async_copy(src, dst, ls.at[take(locals_)])
        when(cond, lambda: cp.start())
        return lambda: when(cond, lambda: cp.wait())

    def rows(start, n):
        return pl.ds(pl.multiple_of(start, 128), n)

    def loop(lo, hi, fn):
        def step(i, _):
            fn(i)
            return 0

        lax.fori_loop(lo, hi, step, 0)

    W, IN = {Q: w_q, O: w_o}, {Q: in_q, O: in_o}
    G, FIN = {O: w_o}, {O: fin_o}
    for k in range(2):
        half = pl.ds(k, 1)
        u, d = (U0, U1)[k], (D0, D1)[k]
        W[u], W[d] = w_u.at[half], w_d.at[half]
        IN[u], IN[d] = in_u.at[half], in_d.at[half]
        G[u], G[d] = w_u.at[half], g_d.at[half]
        FIN[u], FIN[d] = fin_u.at[half], fin_d.at[half]
    for p in range(3):
        G[Q0 + p] = g_q.at[:, p]
        FIN[Q0 + p] = fin_q.at[:, p]
    HC = 6 * HEAD_DIM
    NP = HC // 128
    NC = 2 * R // C
    HB = R // C

    barrier = pltpu.get_barrier_semaphore()
    wd = wx + 4 - 8 * yy
    plane = [(wc, z), (wx, z), (wy, z), (wd, z)]
    plane += [(v + 1 - 2 * c, z) for v in (wx, wy, wd)]
    partners = plane + [(w, z1), (w, z2), (w, z3), (wc, z2), (wc, z3)]
    for dev in partners:
        pl.semaphore_signal(barrier, inc=1, device_id=dev, device_id_type=MESH)
    pl.semaphore_wait(barrier, len(partners))

    w_native = {}
    w_sent = {g: [] for g, _, _ in GEO}
    wz_r = {g: take(recvs, 2) for g, _, _ in GEO}
    wxy_r = {g: take(recvs, 6) for g, _, _ in GEO}

    def weights_out(g, group=pending):
        src = IN[g].at[:, yy, xx]
        dst = W[g].at[:, h, yy, xx]
        send(src, dst, wz_r[g] + h, (w, entry), home, group)
        send(src, dst, wz_r[g] + h, (w, z1), home, group)

    def weights_native(g):
        w_native[g] = local(IN[g], W[g].at[:, h], home)

    def foreign(s):
        return jnp.logical_not(jnp.logical_and(home, h == s))

    def weights_spread(g):
        for s in range(2):
            piece = W[g].at[:, s, yy, xx]
            recv(piece, wz_r[g] + s, foreign(s))
            for j, dev in enumerate((wx, wy)):
                send(piece, piece, wxy_r[g] + 3 * s + j, (dev, z), foreign(s), w_sent[g])
            send(piece, piece, wz_r[g] + s, (w, far), is_entry, w_sent[g])

    def weights_relay(g):
        piece = W[g].at[:, 0, yy, 1 - xx]
        recv(piece, wxy_r[g], foreign(0))
        send(piece, piece, wxy_r[g] + 2, (wy, z), foreign(0), w_sent[g])
        piece = W[g].at[:, 1, 1 - yy, xx]
        recv(piece, wxy_r[g] + 4, foreign(1))
        send(piece, piece, wxy_r[g] + 5, (wx, z), foreign(1), w_sent[g])

    def weights_wait(g):
        w_native[g]()
        recv(W[g].at[:, 0, 1 - yy, xx], wxy_r[g] + 1, foreign(0))
        recv(W[g].at[:, 0, 1 - yy, 1 - xx], wxy_r[g] + 2, foreign(0))
        recv(W[g].at[:, 1, yy, 1 - xx], wxy_r[g] + 3, foreign(1))
        recv(W[g].at[:, 1, 1 - yy, 1 - xx], wxy_r[g] + 5, foreign(1))

    bs_own[...] = jnp.full(bs_own.shape, bs_ref[0], jnp.int32)
    bs_r = take(recvs)
    send(bs_own, bs_buf, bs_r, (wc, z))

    halves = [pl.ds(k * (R // 2), R // 2) for k in range(2)]

    def block(ref, b, k):
        return ref.at[pl.ds(pl.multiple_of(R * b + k * (R // 2), 128), R // 2)]

    tok_r = take(recvs, 6)
    tok_local = local(tok_ref, x.at[pl.ds(pl.multiple_of(R * c, 128), R)], home)
    slot = (1 - c) * (4 - z)
    zt = (1 - c) + c * (z + 2)
    halo_src = jnp.logical_and(c == 1, z == 2)
    def tokens_out(k):
        src = tok_ref.at[halves[k]]
        send(src, block(x, slot, k), tok_r + 2 * slot + k, (wc, zt), away)

    def tokens_home():
        for k in range(2):
            send(tok_ref.at[halves[k]], block(x, c, k), tok_r + 2 * c + k, (wc, z), home)
        for g, _, _ in GEO:
            weights_native(g)

    def halo_out(k):
        send(tok_ref.at[halves[k]], block(x, 2, k), tok_r + 4 + k, (w, 3), halo_src)

    params = (g1_ref, s1_ref, ob_ref, g2_ref, s2_ref, db_ref, upb_ref)

    def param(k):
        return params[k][...].astype(F32).reshape(1, D)

    bias_r = take(recvs, 2)
    bias_sent = []

    def place():
        row_i = lax.broadcasted_iota(jnp.int32, (HC // 2, HC), 0)
        col_i = lax.broadcasted_iota(jnp.int32, (HC // 2, HC), 1)
        source = lax.div(col_i, 128) * HEAD_DIM + lax.rem(col_i, HEAD_DIM)
        mine = lax.div(lax.rem(col_i, 128), HEAD_DIM) == h
        return jnp.logical_and(source == row_i, mine).astype(F32)

    def biases_out():
        bias_own[...] = jnp.zeros(bias_own.shape, F32)
        bias_own[0:3, 0:HC] = mm(qkvb_ref[...], place().astype(BF16))
        bias_own[3:4, pl.ds(pl.multiple_of(h * D, 128), D)] = param(6)
        for dz in (entry, z1, far):
            send(bias_own, biases.at[h], bias_r + h, (w, dz), home, bias_sent)

        @pl.when(home)
        def _():
            biases[h] = bias_own[...]

        @pl.when(h == 0)
        def _():
            x[pl.ds(2 * R, R), :] = jnp.zeros((R, D), BF16)

    gain1, shift1 = param(0), param(1)

    def norm_block(b):
        def step(i):
            r = rows(R * b + i * C, C)
            normed, _inv = norm_stats(x[r, :].astype(F32))
            a1[r, :] = (normed * gain1 + shift1).astype(BF16)

        loop(0, R // C, step)

    def masks():
        recv(bs_buf, bs_r)
        pick = (t == c).astype(jnp.int32)
        bl = bs_own[0:1, :] * pick + bs_buf[0:1, :] * (1 - pick)
        bl = jnp.concatenate([bl, bl], axis=1)

        def block_of(v):
            return jnp.where(
                bl == 4,
                lax.shift_right_logical(v, 2),
                jnp.where(bl == 8, lax.shift_right_logical(v, 3), lax.shift_right_logical(v, 4)),
            )

        key_no = block_of(lax.broadcasted_iota(jnp.int32, (T, 2 * T), 0))
        row_no = block_of(lax.rem(lax.broadcasted_iota(jnp.int32, (T, 2 * T), 1), T))
        m_same[...] = jnp.where(key_no == row_no, 0.0, NEG)
        m_lt[...] = jnp.where(key_no < row_no, 0.0, NEG)
        m_le[...] = jnp.where(key_no <= row_no, 0.0, NEG)

    def norm_local():
        tok_local()
        for k in range(2):
            recv(block(x, 1 - c, k), tok_r + 2 * (1 - c) + k, away)
        norm_block(t)

    takes_halo = jnp.logical_and(c == 1, h == 1)
    feeds = jnp.logical_and(c == 1, z == 1)

    def halo_pass(k):
        recv(block(x, 2, k), tok_r + 4 + k, takes_halo)
        send(block(x, 2, k), block(x, 1, k), tok_r + 2 + k, (w, 0), feeds)
        send(block(x, 2, k), block(x, 2, k), tok_r + 4 + k, (wc, z), takes_halo)

    def tokens_pass(k):
        recv(block(x, c, k), tok_r + 2 * c + k, away)
        send(block(x, c, k), block(x, c, k), tok_r + 2 * c + k, (wc, z), away)

    cot_r = take(recvs, 4)
    cot_local = []

    def cotangents_out(k):
        src = cot_ref.at[halves[k]]
        send(src, block(cot, c, k), cot_r + 2 * c + k, (wc, z), home)
        send(src, block(cot, 1 - c, k), cot_r + 2 * (1 - c) + k, (wc, z2), away)
        cot_local.append(local(src, block(cot, c, k), home))

    def norm_other():
        for k in range(2):
            recv(block(x, 1 - c, k), tok_r + 2 * (1 - c) + k, home)
        norm_block(1 - t)

    def norm_halo():
        for k in range(2):
            recv(block(x, 2, k), tok_r + 4 + k, jnp.logical_and(c == 0, h == 1))
        norm_block(2)

    def biases_in():
        recv(biases.at[0], bias_r, foreign(0))
        recv(biases.at[1], bias_r + 1, foreign(1))
        sent(bias_sent)
        bias_own[...] = biases[0] + biases[1]


    def wq(j):
        return w_q[3 * j : 3 * j + 3].reshape(HC, D)

    def cos_sin(place, n):
        r = rows(place, n)
        return cos_ref[r, :], sin_ref[r, :]

    def project(i, halo):
        r = rows(i * C, C)
        a = a1[r, :]
        place = (i * C - 2 * R) if halo else (R * h + lax.rem(i * C, R))
        cs, sn = cos_sin(place, C)
        if not halo:
            qv = mm_nt(a, wq(0)) + bias_own[0:1, :HC]
            for p in range(NP):
                v = qv[:, p * 128 : p * 128 + 128]
                qs[p, r, :] = ((v * cs + swap_halves(v) * sn) * 0.125).astype(BF16)
        kv = mm_nt(a, wq(1)) + bias_own[1:2, :HC]
        for p in range(NP):
            v = kv[:, p * 128 : p * 128 + 128]
            ks[p, r, :] = (v * cs + swap_halves(v) * sn).astype(BF16)
        vv = mm_nt(a, wq(2)) + bias_own[2:3, :HC]
        for p in range(NP):
            vs[p, r, :] = vv[:, p * 128 : p * 128 + 128].astype(BF16)

    def project_block(b):
        loop(0, HB, lambda i: project(HB * b + i, False))

    def project_halo():
        loop(NC, NC + HB, lambda i: project(i, True))

    halo_bias = jnp.where(h == 1, 0.0, NEG).astype(F32)
    lane = lax.broadcasted_iota(jnp.int32, (1, 128), 1)
    lo_f = (lane < 64).astype(F32)
    lo_mask = lo_f.astype(BF16)
    hi_mask = (1.0 - lo_f).astype(BF16)

    def both_heads(v):
        return jnp.concatenate([v * lo_mask, v * hi_mask], axis=0)

    def one_of_each(v):
        return v[:T] * lo_f + v[T:] * (1.0 - lo_f)

    def key_parts(b, i):
        parts = []
        if b == 0:
            parts.append((T * i, T, m_same))
        if i > 0:
            parts.append((R, T * i, None))
        parts.append((R + T * i, T, m_lt if b == 0 else m_le))
        parts.append((2 * R, R, halo_bias))
        return parts

    def scores_of(p, part, qm):
        start, n, mask = part
        sc = mm_nt(ks[p, pl.ds(start, n), :], qm)
        if mask is None:
            return sc
        if mask is halo_bias:
            return sc + halo_bias
        return sc + mask[...]

    chunks = [(b, i) for b in range(2) for i in range(R // T)]

    def attend(p, n):
        for b, i in chunks[n : n + 1]:
            r = pl.ds(R * b + T * i, T)
            qm = both_heads(qs[p, r, :])
            parts = key_parts(b, i)
            sc = [scores_of(p, part, qm) for part in parts]
            top = None
            for v in sc:
                m = jnp.max(v, axis=0, keepdims=True)
                top = m if top is None else jnp.maximum(top, m)
            total, out = None, None
            for part, v in zip(parts, sc):
                e = jnp.exp(v - top)
                l = jnp.sum(e, axis=0, keepdims=True)
                o = mm_tn(vs[p, pl.ds(part[0], part[1]), :], e.astype(BF16))
                total = l if total is None else total + l
                out = o if out is None else out + o
            out = out / total
            att[p, r, :] = one_of_each(out.T).astype(BF16)
            lse[p, n] = top + jnp.log(total)

    e1_r = take(recvs, 4)
    e1_s = take(sends, 4)
    def swap_out(i, dst, si, ri):
        r = rows(i * C, C)
        remote(e1s.at[r], dst.at[r], si + i, ri + i, (wc, z)).start()

    def swap_in(i, dst, ri):
        r = rows(i * C, C)
        remote(dst.at[r], dst.at[r], 0, ri + i, (wc, z)).wait_recv()

    def swap_done(i, dst, si):
        r = rows(i * C, C)
        remote(e1s.at[r], dst.at[r], si + i, 0, (wc, z)).wait_send()

    def pairs(ref, r):
        return jnp.concatenate([ref[p, r, :] for p in range(NP)], axis=1)

    def out_project(i):
        r = rows(i * C, C)
        e1s[r, :] = mm(pairs(att, r), w_o[...].reshape(HC, D)).astype(BF16)
        swap_out(i, e1r, e1_s, e1_r)


    def clear():
        sm[...] = jnp.zeros(sm.shape, F32)
        ub[...] = jnp.zeros(ub.shape, F32)
        qb[...] = jnp.zeros(qb.shape, F32)

    out_bias, gain2, shift2, down_bias = param(2), param(3), param(4), param(5)
    KG = float(np.sqrt(2.0 / np.pi))

    def wu(s):
        return jnp.concatenate([w_u[0, s].reshape(D // 2, D), w_u[1, s].reshape(D // 2, D)], axis=0)

    def wd(s):
        return jnp.concatenate([w_d[0, s].reshape(D // 2, D), w_d[1, s].reshape(D // 2, D)], axis=0)

    def feed(i):
        r = rows(i * C, C)
        swap_in(i, e1r, e1_r)
        hv = x[r, :].astype(F32) + e1s[r, :].astype(F32) + e1r[r, :].astype(F32) + out_bias
        hid[r, :] = hv
        normed, _inv = norm_stats(hv)
        act = (normed * gain2 + shift2).astype(BF16)
        a2[r, :] = act
        for s in range(2):
            cols = pl.ds(s * D, D)
            u = mm(act, wu(s)) + bias_own[3:4, s * D : (s + 1) * D]
            u2 = u * u
            th = jnp.tanh(KG * u * (1.0 + 0.044715 * u2))
            half = 0.5 * (1.0 + th)
            gelu[r, cols] = (u * half).astype(BF16)
            slope = half + 0.5 * u * (1.0 - th * th) * (KG * (1.0 + 3 * 0.044715 * u2))
            gp[r, cols] = slope.astype(BF16)

    def cot_pass(k):
        cot_local[k]()
        recv(block(cot, c, k), cot_r + 2 * c + k, away)
        send(block(cot, c, k), block(cot, c, k), cot_r + 2 * c + k, (wc, z), away)

    def cot_in():
        for k in range(2):
            recv(block(cot, 1 - c, k), cot_r + 2 * (1 - c) + k)

    ra_r = {g: take(recvs, 2) for g, _, _ in RED}
    rb_r = {g: take(recvs, 2) for g, _, _ in RED}
    rc_r = {g: take(recvs, 2) for g, _, _ in RED}
    rd_r = {g: take(recvs, 2) for g, _, _ in RED}
    fin_r = {g: take(recvs, 4) for g, _, _ in RED}
    fin_local = {}
    size = {g: (n, r) for g, n, r in RED}
    turn = {g: k % 2 for k, (g, _, _) in enumerate(RED)}

    def add(dst, src):
        dst[...] = (dst[...].astype(F32) + src[...].astype(F32)).astype(BF16)

    def reduce_a(g):
        send(G[g].at[:, 0, :, 1 - xx], RA[g].at[0], ra_r[g], (wx, z))
        send(G[g].at[:, 1, 1 - yy, :], RA[g].at[1], ra_r[g] + 1, (wy, z))

    def reduce_b(g):
        n, r = size[g]
        recv(RA[g].at[0], ra_r[g])
        for k in range(n):
            add(G[g].at[k, 0, 1 - yy, xx], RA[g].at[0, k, 1 - yy])
        send(G[g].at[:, 0, 1 - yy, xx], RB[g].at[0], rb_r[g], (wy, z))
        recv(RA[g].at[1], ra_r[g] + 1)
        for k in range(n):
            add(G[g].at[k, 1, yy, 1 - xx], RA[g].at[1, k, 1 - xx])
        send(G[g].at[:, 1, yy, 1 - xx], RB[g].at[1], rb_r[g] + 1, (wx, z))
        for k in range(n):
            add(G[g].at[k, 0, yy, xx], RA[g].at[0, k, yy])
            add(G[g].at[k, 1, yy, xx], RA[g].at[1, k, xx])

    def reduce_c(g):
        n, r = size[g]
        for s in range(2):
            recv(RB[g].at[s], rb_r[g] + s)
            for k in range(n):
                add(G[g].at[k, s, yy, xx], RB[g].at[s, k])
            piece = G[g].at[:, s, yy, xx]
            if g in DIRECT:
                at = (w, 2 * c + s)
                send(piece, RC[g].at[0], rc_r[g], at, is_far)
                send(piece, RD[g].at[1], rd_r[g] + 1, at, is_entry)
            else:
                send(piece, RC[g].at[s], rc_r[g] + s, (w, entry), is_far)
            send(piece, RD[g].at[0], rd_r[g], (w, z1), jnp.logical_and(home, h == 1 - s))

    def reduce_d(g):
        n, r = size[g]
        if g in DIRECT:
            return
        for s in range(2):
            recv(RC[g].at[s], rc_r[g] + s, is_entry)

            @pl.when(is_entry)
            def _():
                for k in range(n):
                    add(G[g].at[k, s, yy, xx], RC[g].at[s, k])

            send(G[g].at[:, s, yy, xx], RD[g].at[1], rd_r[g] + 1, (w, 2 * c + s), is_entry)

    def reduce_e(g):
        n, r = size[g]
        recv(RD[g].at[0], rd_r[g], home)
        recv(RD[g].at[1], rd_r[g] + 1, home)
        if g in DIRECT:
            recv(RC[g].at[0], rc_r[g], home)

        @pl.when(home)
        def _():
            for k in range(n):
                dst = G[g].at[k, h, yy, xx]
                v = dst[...].astype(F32) + RD[g][0, k].astype(F32) + RD[g][1, k].astype(F32)
                if g in DIRECT:
                    v = v + RC[g][0, k].astype(F32)
                dst[...] = v.astype(BF16)

        piece = G[g].at[:, h, yy, xx]
        out = FIN[g].at[:, yy, xx]
        fin_local[g] = local(piece, out, home)
        for j, dev in enumerate((wx, wy)):
            send(piece, out, fin_r[g] + j, (dev, z), home)
        send(piece, out, fin_r[g] + 3, (wc, z), home)

    def reduce_f(g):
        for j, (py, px) in enumerate(((yy, 1 - xx), (1 - yy, xx))):
            piece = FIN[g].at[:, py, px]
            recv(piece, fin_r[g] + j, home)
            if j == turn[g]:
                send(piece, piece, fin_r[g] + 2, ((wy, wx)[j], z), home)
            send(piece, piece, fin_r[g] + j, (wc, z), home)

    def reduce_g(g):
        piece = FIN[g].at[:, 1 - yy, 1 - xx]
        recv(piece, fin_r[g] + 2, home)
        send(piece, piece, fin_r[g] + 2, (wc, z), home)

    def reduce_h(g):
        fin_local[g]()
        for j, (py, px) in enumerate(((yy, 1 - xx), (1 - yy, xx), (1 - yy, 1 - xx), (yy, xx))):
            recv(FIN[g].at[:, py, px], fin_r[g] + j, away)

    def grad_down(half, s):
        cols = pl.ds(pl.multiple_of(s * D + half * (D // 2), 128), D // 2)
        g = mm_tn(gelu[:, cols], cot[...])
        g_d[half, s] = g.astype(BF16).reshape(2, 2, 96, D)

    def grad_up(half, s):
        g = mm_tn(
            a2[:, half * (D // 2) : (half + 1) * (D // 2)],
            gp[:, pl.ds(pl.multiple_of(s * D, 128), D)],
        )
        w_u[half, s] = g.astype(BF16).reshape(2, 2, 96, D)

    def grads_down(half):
        loop(0, 2, lambda s: grad_down(half, s))

    def grads_up(half):
        sent(w_sent[U0 + half])
        loop(0, 2, lambda s: grad_up(half, s))

    e3_r, e3_s = take(recvs, 4), take(sends, 4)

    def back_up(i):
        r = rows(i * C, C)
        cv = cot[r, :]
        out = None
        for s in range(2):
            cols = pl.ds(s * D, D)
            gu = (mm_nt(cv, wd(s)) * gp[r, cols].astype(F32)).astype(BF16)
            gp[r, cols] = gu
            ub[0:1, cols] += jnp.sum(gu.astype(F32), axis=0, keepdims=True)
            o = mm_nt(gu, wu(s))
            out = o if out is None else out + o
        e1s[r, :] = out.astype(BF16)
        swap_out(i, e3r, e3_s, e3_r)

    def backs_up():
        loop(0, NC, lambda i: swap_done(i, e1r, e1_s))
        loop(0, NC, back_up)

    e2_r, e2_s = take(recvs, 2), take(sends, 2)

    def down_of(r):
        return mm(gelu[r, 0:D], wd(0)) + mm(gelu[r, D : 2 * D], wd(1))

    def down_other(i):
        r = rows(R * (1 - c) + i * C, C)
        d = rows(i * C, C)
        e2s[d, :] = down_of(r).astype(BF16)
        remote(e2s.at[d], e2r.at[d], e2_s + i, e2_r + i, (wc, z)).start()

    def down_own(i):
        r = rows(R * c + i * C, C)
        d = rows(i * C, C)
        part = down_of(r)
        remote(e2r.at[d], e2r.at[d], 0, e2_r + i, (wc, z)).wait_recv()
        y = hid[r, :] + part + e2r[d, :].astype(F32) + down_bias
        ybuf[d, :] = y.astype(BF16)
        sm[5:6, :] += jnp.sum(cot[r, :].astype(F32), axis=0, keepdims=True)

    z_orig = 2 * c + h
    y_r = take(recvs)
    y_local = []

    def down_mine():
        loop(0, HB, down_own)
        y_local.append(local(ybuf, act_out, home))
        send(ybuf, act_out, y_r, (wc, z_orig), away)

    def norm2_back(i):
        r = rows(i * C, C)
        swap_in(i, e3r, e3_r)
        g2 = e1s[r, :].astype(F32) + e3r[r, :].astype(F32)
        normed, inv = norm_stats(hid[r, :])
        gh = cot[r, :].astype(F32) + norm_back(g2, normed, inv, gain2)
        hid[r, :] = gh
        own = (lax.div(i, HB) == c).astype(F32)
        sm[3:4, :] += own * jnp.sum(g2 * normed, axis=0, keepdims=True)
        sm[4:5, :] += own * jnp.sum(g2, axis=0, keepdims=True)
        sm[2:3, :] += own * jnp.sum(gh, axis=0, keepdims=True)
        swap_done(i, e3r, e3_s)
        br = gh.astype(BF16)
        e1s[r, :] = br
        a2[r, 0:HC] = mm_nt(br, w_o[...].reshape(HC, D)).astype(BF16)

    def grad_out():
        everything = pl.ds(0, 2 * R)
        sent(w_sent[O])
        g_out = mm_tn(pairs(att, everything), e1s[...])
        w_o[...] = g_out.astype(BF16).reshape(3, 2, 2, 2, 16, D)

    def attend_back(p, n):
        if n == 0:
            dk[...] = jnp.zeros(dk.shape, F32)
            dv[...] = jnp.zeros(dv.shape, F32)
        for b, i in chunks[n : n + 1]:
            r = pl.ds(R * b + T * i, T)
            qm = both_heads(qs[p, r, :])
            gm = both_heads(a2[r, p * 128 : p * 128 + 128])
            parts = key_parts(b, i)
            log_total = lse[p, n]
            delta, probs, gprobs = None, [], []
            for part in parts:
                pr = jnp.exp(scores_of(p, part, qm) - log_total)
                dp = mm_nt(vs[p, pl.ds(part[0], part[1]), :], gm)
                dl = jnp.sum(pr * dp, axis=0, keepdims=True)
                delta = dl if delta is None else delta + dl
                probs.append(pr)
                gprobs.append(dp)
            dq = None
            for part, pr, dp in zip(parts, probs, gprobs):
                k = pl.ds(part[0], part[1])
                ds = (pr * (dp - delta)).astype(BF16)
                dv[k, :] += mm(pr.astype(BF16), gm)
                dk[k, :] += mm(ds, qm)
                d = mm_tn(ks[p, k, :], ds)
                dq = d if dq is None else dq + d
            dq = one_of_each(dq.T) * 0.125
            cs, sn = cos_sin(R * h + T * i, T)
            dq = (dq * cs - swap_halves(dq) * sn).astype(BF16)
            qs[p, r, :] = dq

    def attend_end(p):
        for b in range(3):
            cs, sn = cos_sin(R * h if b < 2 else 0, R)
            r = pl.ds(R * b, R)
            v = dk[r, :]
            ks[p, r, :] = (v * cs - swap_halves(v) * sn).astype(BF16)
            vs[p, r, :] = dv[r, :].astype(BF16)

    def grad_qkv(p):
        r, o = pl.ds(0, 2 * R), pl.ds(2 * R, R)
        lhs = jnp.concatenate([qs[p, r, :], ks[p, r, :], vs[p, r, :]], axis=1)
        over = jnp.concatenate([ks[p, o, :], vs[p, o, :]], axis=1)
        g = mm_tn(lhs, a1[r, :])
        g_over = mm_tn(over, a1[o, :])
        g_q[0, p] = g[:128].astype(BF16).reshape(2, 2, 2, 16, D)
        for j in range(2):
            part = g[128 * (j + 1) : 128 * (j + 2)] + g_over[128 * j : 128 * (j + 1)]
            g_q[j + 1, p] = part.astype(BF16).reshape(2, 2, 2, 16, D)
        cols = pl.ds(128 * p, 128)
        qb[0:1, cols] = jnp.sum(qs[p, r, :].astype(F32), axis=0, keepdims=True)
        qb[1:2, cols] = jnp.sum(ks[p].astype(F32), axis=0, keepdims=True)
        qb[2:3, cols] = jnp.sum(vs[p].astype(F32), axis=0, keepdims=True)

    def back_qkv(r, halo):
        g = mm(pairs(ks, r), wq(1)) + mm(pairs(vs, r), wq(2))
        return g if halo else g + mm(pairs(qs, r), wq(0))

    hal_r, hal_s = take(recvs, 2), take(sends, 2)
    halz_r = take(recvs, 2)
    e4_r, e4_s = take(recvs, 2), take(sends, 2)

    def halo_back(i):
        d = rows(i * C, C)
        hals[d, :] = back_qkv(rows(2 * R + i * C, C), True).astype(BF16)

        @pl.when(c == 0)
        def _():
            remote(hals.at[d], halr.at[d], hal_s + i, hal_r + i, (wc, z)).start()

    def halos_back():
        loop(0, HB, halo_back)

    def other_back(i):
        d = rows(i * C, C)
        e2s[d, :] = back_qkv(rows(R * (1 - c) + i * C, C), False).astype(BF16)
        remote(e2s.at[d], e4r.at[d], e4_s + i, e4_r + i, (wc, z)).start()

    def others_back():
        loop(0, HB, lambda i: remote(
            e2s.at[rows(i * C, C)], e2r.at[rows(i * C, C)], e2_s + i, 0, (wc, z)).wait_send())
        loop(0, HB, other_back)

    def halo_sum(k):
        d = pl.ds(k * C, C)
        recv(halr.at[d], hal_r + k, c == 1)

        @pl.when(c == 1)
        def _():
            add(hals.at[d], halr.at[d])

        send(hals.at[d], halz.at[d], halz_r + k, (w, z1), jnp.logical_and(c == 1, h == 1))

    def own_back(i):
        tg[rows(i * C, C), :] = back_qkv(rows(R * c + i * C, C), False)

    def owns_back():
        loop(0, HB, own_back)

        @pl.when(jnp.logical_not(gets))
        def _():
            halz[...] = jnp.zeros(halz.shape, BF16)

    gets = jnp.logical_and(c == 1, h == 0)
    t_r = take(recvs, 2)

    def norm1_back(i):
        d = pl.ds(i * C, C)
        r = rows(R * c + i * C, C)
        recv(halz.at[d], halz_r + i, gets)
        remote(e4r.at[d], e4r.at[d], 0, e4_r + i, (wc, z)).wait_recv()
        g1 = tg[d, :] + e4r[d, :].astype(F32) + halz[d, :].astype(F32)
        normed, inv = norm_stats(x[r, :].astype(F32))
        out = hid[r, :] + norm_back(g1, normed, inv, gain1)
        sm[0:1, :] += jnp.sum(g1 * normed, axis=0, keepdims=True)
        sm[1:2, :] += jnp.sum(g1, axis=0, keepdims=True)
        e1r[d, :] = out.astype(BF16)
        send(e1r.at[d], tgrad_out.at[d], t_r + i, (wc, z_orig), away)
        t_local.append(local(e1r.at[d], tgrad_out.at[d], home))

    t_local = []

    me = lax.rem(w, 8)
    base = w - me
    sm_r, sm2_r = take(recvs, 8), take(recvs, 4)

    def small_out_plane():
        cf = c.astype(F32)
        for j in range(3):
            sm[6 + j : 7 + j, 0:HC] = qb[j : j + 1, :] * (1.0 - cf)
            sm[6 + j : 7 + j, HC : 2 * HC] = qb[j : j + 1, :] * cf
        for s in range(2):
            sm[9 + s : 10 + s, :] = ub[0:1, s * D : (s + 1) * D] * (1.0 - cf)
            sm[11 + s : 12 + s, :] = ub[0:1, s * D : (s + 1) * D] * cf
        smr[me] = sm[...]
        for dev in plane:
            send(smr.at[me], smr.at[me], sm_r + me, dev)

    def small_out_z():
        for dev, _ in plane:
            other = dev - base
            recv(smr.at[other], sm_r + other)
        total = smr[0]
        for k in range(1, 8):
            total = total + smr[k]
        smz[z] = total
        for dev in (z1, z2, z3):
            send(smz.at[z], smz.at[z], sm2_r + z, (w, dev))

    def small_end():
        for dev in (z1, z2, z3):
            recv(smz.at[dev], sm2_r + dev)
        total = smz[0] + smz[1] + smz[2] + smz[3]
        sm[...] = total
        small_out[...] = total
        small_out[9:10, :] = sm[pl.ds(9 + z, 1), :]
        mine = sm[6:9, pl.ds(pl.multiple_of(HC * t, 128), HC)]
        small_out[6:9, 0 : HC // 2] = lax.dot_general(
            mine, place(), (((1,), (1,)), ((), ())), precision=lax.Precision.HIGHEST,
            preferred_element_type=F32,
        )

    weights_out(Q)
    biases_out()
    halo_out(0)
    tokens_out(0)
    halo_out(1)
    weights_spread(Q)
    halo_pass(0)
    tokens_out(1)
    tokens_pass(0)
    weights_out(O)
    tokens_home()
    weights_relay(Q)
    norm_local()
    weights_spread(O)
    masks()
    halo_pass(1)
    weights_out(U0)
    tokens_pass(1)
    weights_relay(O)
    weights_spread(U0)
    norm_halo()
    biases_in()
    weights_wait(Q)
    weights_out(U1)
    project_block(t)
    norm_other()
    weights_out(D0)
    project_block(1 - t)
    weights_spread(U1)
    project_halo()
    attend(0, 0)
    attend(0, 1)
    clear()
    cotangents_out(0)
    weights_wait(O)
    attend(0, 2)
    attend(0, 3)
    attend(0, 4)
    attend(0, 5)
    weights_relay(U0)
    attend(0, 6)
    weights_out(D1)
    attend(0, 7)
    attend(1, 0)
    attend(1, 1)
    attend(1, 2)
    attend(1, 3)
    weights_relay(U1)
    weights_spread(D0)
    attend(1, 4)
    attend(1, 5)
    attend(1, 6)
    attend(1, 7)
    attend(2, 0)
    attend(2, 1)
    attend(2, 2)
    cotangents_out(1)
    attend(2, 3)
    weights_wait(U0)
    attend(2, 4)
    attend(2, 5)
    attend(2, 6)
    weights_spread(D1)
    attend(2, 7)
    loop(0, NC, out_project)
    weights_relay(D0)
    weights_wait(U1)
    loop(0, NC, feed)
    weights_relay(D1)
    cot_pass(0)
    cot_pass(1)
    weights_wait(D0)
    cot_in()
    grads_down(0)
    weights_wait(D1)
    reduce_a(D0)
    loop(0, HB, down_other)
    grads_down(1)
    reduce_a(D1)
    backs_up()
    reduce_b(D0)
    grads_up(0)
    reduce_a(U0)
    down_mine()
    grads_up(1)
    loop(0, NC, norm2_back)
    attend_back(0, 0)
    reduce_a(U1)
    attend_back(0, 1)
    reduce_b(D1)
    attend_back(0, 2)
    attend_back(0, 3)
    attend_back(0, 4)
    attend_back(0, 5)
    reduce_c(D0)
    reduce_b(U0)
    attend_back(0, 6)
    attend_back(0, 7)
    attend_end(0)
    grad_out()
    attend_back(1, 0)
    reduce_a(O)
    attend_back(1, 1)
    reduce_c(D1)
    grad_qkv(0)
    attend_back(1, 2)
    attend_back(1, 3)
    attend_back(1, 4)
    reduce_b(U1)
    attend_back(1, 5)
    attend_back(1, 6)
    attend_back(1, 7)
    attend_end(1)
    attend_back(2, 0)
    reduce_b(O)
    reduce_d(D0)
    attend_back(2, 1)
    reduce_a(Q0)
    reduce_c(U1)
    attend_back(2, 2)
    grad_qkv(1)
    reduce_a(Q1)
    reduce_c(O)
    reduce_d(D1)
    attend_back(2, 3)
    reduce_e(D0)
    reduce_c(U0)
    attend_back(2, 4)
    attend_back(2, 5)
    attend_back(2, 6)
    attend_back(2, 7)
    attend_end(2)
    reduce_b(Q1)
    reduce_d(U1)
    reduce_b(Q0)
    halos_back()
    halo_sum(0)
    grad_qkv(2)
    reduce_e(U1)
    reduce_e(O)
    reduce_c(Q0)
    reduce_e(D1)
    halo_sum(1)
    reduce_a(Q2)
    reduce_c(Q1)
    reduce_f(O)
    others_back()
    reduce_d(U0)
    reduce_f(D0)
    reduce_b(Q2)
    reduce_e(Q0)
    reduce_g(D0)
    reduce_e(U0)
    reduce_e(Q1)
    owns_back()
    reduce_c(Q2)
    reduce_f(Q0)
    norm1_back(0)
    reduce_e(Q2)
    norm1_back(1)
    small_out_plane()
    reduce_f(Q1)
    reduce_f(Q2)
    reduce_g(O)
    reduce_g(Q0)
    reduce_g(Q2)
    reduce_f(D1)
    small_out_z()
    reduce_g(Q1)
    reduce_f(U0)
    reduce_f(U1)
    reduce_g(U0)
    reduce_g(D1)
    reduce_g(U1)
    small_end()
    for g, _, _ in RED:
        reduce_h(g)
    recv(act_out, y_r, away)
    y_local[0]()
    for k in range(HB):
        d = pl.ds(k * C, C)
        recv(tgrad_out.at[d], t_r + k, away)
        t_local[k]()
    loop(0, HB, lambda i: remote(
        e2s.at[rows(i * C, C)], e4r.at[rows(i * C, C)], e4_s + i, 0, (wc, z)).wait_send())

    @pl.when(c == 0)
    def _():
        for k in range(HB):
            d = pl.ds(k * C, C)
            remote(hals.at[d], halr.at[d], hal_s + k, 0, (wc, z)).wait_send()

    sent(w_sent[Q])
    sent(w_sent[D0])
    sent(w_sent[D1])
    sent(pending)
    counts = (next(sends), next(recvs), next(locals_))
    assert counts[0] <= ss.shape[0] and counts[1] <= rs.shape[0] and counts[2] <= ls.shape[0], counts


def shards(
    tokens, block_size, ln1_gain, ln1_shift, qkv_weight, qkv_bias, out_weight, out_bias,
    ln2_gain, ln2_shift, up_weight, up_bias, down_weight, down_bias, cotangent, groups,
):
    R, D = tokens.shape
    local_width = qkv_weight.shape[2]
    HC = 2 * local_width
    FC = 2 * up_weight.shape[1]
    cos, sin = tables(2 * R)
    wq = jnp.transpose(qkv_weight, (1, 2, 0)).reshape(9, 2, 2, 16, D)
    wo = out_weight.reshape(3, 2, 2, 16, D)
    wu = up_weight.reshape(2, 2, 2, 96, D)
    wdn = down_weight.reshape(2, 2, 2, 96, D)
    anyspec = pl.BlockSpec(memory_space=pl.ANY)
    vspec = pl.BlockSpec(memory_space=pltpu.VMEM)
    sds = jax.ShapeDtypeStruct
    fins = [sds((3, 3, 2, 2, 16, D), BF16), sds((3, 2, 2, 16, D), BF16)]
    fins += [sds((2, 2, 2, 96, D), BF16)] * 2
    V = pltpu.VMEM
    weights = [V((n, 2, 2, 2, r, D), BF16) for n, r in ((9, 16), (3, 16), (2, 96), (2, 96))]
    recvs = []
    for _, n, r in RED:
        recvs += [
            V((2, n, 2, r, D), BF16),
            V((2, n, r, D), BF16),
            V((2, n, r, D), BF16),
            V((2, n, r, D), BF16),
        ]
    NP = HC // 128
    outs = pl.pallas_call(
        layer_kernel,
        out_shape=[sds((R, D), BF16), sds((R, D), BF16), sds((16, D), F32)] + fins,
        in_specs=[vspec] * 10 + [pl.BlockSpec(memory_space=pltpu.SMEM)] + [anyspec] * 6,
        out_specs=[anyspec, anyspec, vspec] + [anyspec] * 4,
        scratch_shapes=[
            V((3 * R, D), BF16),
            V((3 * R, D), BF16),
            V((NP, 2 * R, 128), BF16),
            V((NP, 3 * R, 128), BF16),
            V((NP, 3 * R, 128), BF16),
            V((NP, 2 * R, 128), BF16),
            V((NP, 2 * R // T, 1, 2 * T), F32),
            V((2 * R, D), F32),
            V((2 * R, D), BF16),
            V((2 * R, FC), BF16),
            V((2 * R, FC), BF16),
            V((2 * R, D), BF16),
            *weights,
            V((3, 3, 2, 2, 2, 16, D), BF16),
            V((2, 2, 2, 2, 96, D), BF16),
            V((8, FC), F32),
            V((2, 8, FC), F32),
            V((8, 128), jnp.int32),
            V((8, 128), jnp.int32),
            V((T, 2 * T), F32),
            V((T, 2 * T), F32),
            V((T, 2 * T), F32),
            V((2 * R, D), BF16),
            V((2 * R, D), BF16),
            V((R, D), BF16),
            V((R, D), BF16),
            V((2 * R, D), BF16),
            V((R, D), BF16),
            V((R, D), BF16),
            V((R, D), BF16),
            V((R, D), BF16),
            V((R, D), BF16),
            V((R, D), F32),
            V((3 * R, 128), F32),
            V((3 * R, 128), F32),
            *recvs,
            V((16, D), F32),
            V((8, 16, D), F32),
            V((4, 16, D), F32),
            V((8, FC), F32),
            V((8, HC), F32),
            pltpu.SemaphoreType.DMA((260,)),
            pltpu.SemaphoreType.DMA((220,)),
            pltpu.SemaphoreType.DMA((24,)),
        ],
        compiler_params=pltpu.CompilerParams(
            collective_id=0, has_side_effects=True, vmem_limit_bytes=62 * 1024 * 1024
        ),
        name="layer",
    )(
        jnp.asarray(cos), jnp.asarray(sin), ln1_gain, ln1_shift, out_bias, ln2_gain, ln2_shift,
        down_bias, up_bias, qkv_bias, block_size, tokens, cotangent, wq, wo, wu, wdn,
    )
    act, tgrad, small, fq, fo, fu, fd = outs
    grads = [
        jnp.transpose(fq.reshape(3, local_width, D), (2, 0, 1)).astype(F32),
        fo.reshape(local_width, D).astype(F32),
        fu.reshape(D, D).astype(F32),
        fd.reshape(D, D).astype(F32),
    ]
    if groups > 1:
        ids = [[g * 8 + k for g in range(groups)] for k in range(8)]
        grads, small = lax.psum((grads, small), "wide", axis_index_groups=ids)
    gq, go, gu, gd = grads
    qb, ubias = small[6:9, :local_width], small[9]
    return (
        act, tgrad, small[0], small[1], gq, qb, go, small[2], small[3], small[4], gu, ubias, gd, small[5],
    )


def solution(mesh):
    both = P(("wide", "narrow"), None)
    in_specs = (
        both, P("wide"), P(), P(), P(None, None, "narrow"), P(None, "narrow"), P("narrow", None), P(),
        P(), P(), P(None, "narrow"), P("narrow"), P("narrow", None), P(), both,
    )
    out_specs = (
        both, both, P(), P(), P(None, None, "narrow"), P(None, "narrow"), P("narrow", None), P(),
        P(), P(), P(None, "narrow"), P("narrow"), P("narrow", None), P(),
    )
    groups = mesh.shape["wide"] // 8

    def body(*args):
        return shards(*args, groups)

    return jax.shard_map(body, mesh=mesh, in_specs=in_specs, out_specs=out_specs, check_vma=False)
```

```python
import itertools

import jax
import jax.numpy as jnp
import numpy as np
from jax import lax
from jax.experimental import pallas as pl
from jax.experimental.pallas import tpu as pltpu
from jax.sharding import PartitionSpec as P

HEAD_DIM = 64
MESH = pl.DeviceIdType.MESH
F32 = jnp.float32
BF16 = jnp.bfloat16
NEG = -1e30
EPS = 1e-05
T = 128
C = 256
Q, O, U0, U1, D0, D1, Q0, Q1, Q2 = range(9)
GEO = ((Q, 9, 16), (O, 3, 16), (U0, 1, 96), (U1, 1, 96), (D0, 1, 96), (D1, 1, 96))
RED = (
    (D0, 1, 96), (D1, 1, 96), (U0, 1, 96), (U1, 1, 96),
    (O, 3, 16), (Q0, 3, 16), (Q1, 3, 16), (Q2, 3, 16),
)
DIRECT = (O, Q0, Q1, Q2)


def mm(a, b):
    return lax.dot_general(a, b, (((1,), (0,)), ((), ())), preferred_element_type=F32)


def mm_nt(a, b):
    return lax.dot_general(a, b, (((1,), (1,)), ((), ())), preferred_element_type=F32)


def mm_tn(a, b):
    return lax.dot_general(a, b, (((0,), (0,)), ((), ())), preferred_element_type=F32)


def norm_stats(v):
    mean = jnp.mean(v, axis=-1, keepdims=True)
    cen = v - mean
    inv = lax.rsqrt(jnp.mean(cen * cen, axis=-1, keepdims=True) + EPS)
    return cen * inv, inv


def norm_back(grad, normed, inv, gain):
    g = grad * gain
    return inv * (
        g
        - jnp.mean(g, axis=-1, keepdims=True)
        - normed * jnp.mean(g * normed, axis=-1, keepdims=True)
    )


def swap_halves(v):
    lane = lax.broadcasted_iota(jnp.int32, v.shape, 1)
    low = lax.rem(lane, 64) < 32
    return jnp.where(low, pltpu.roll(v, 96, 1), pltpu.roll(v, 32, 1))


def tables(half_len):
    freqs = np.exp(
        np.arange(HEAD_DIM // 2, dtype=np.float32)
        * np.float32(-2.0 * np.log(10000.0) / HEAD_DIM)
    ).astype(np.float32)
    angles = np.arange(half_len, dtype=np.float32)[:, None] * freqs[None, :]
    angles = angles.astype(np.float32)
    cos, sin = np.cos(angles), np.sin(angles)
    return (
        np.concatenate([cos, cos, cos, cos], 1).astype(np.float32),
        np.concatenate([-sin, sin, -sin, sin], 1).astype(np.float32),
    )


def layer_kernel(
    cos_ref, sin_ref, g1_ref, s1_ref, ob_ref, g2_ref, s2_ref, db_ref, upb_ref, qkvb_ref, bs_ref,
    tok_ref, cot_ref, in_q, in_o, in_u, in_d,
    act_out, tgrad_out, small_out, fin_q, fin_o, fin_u, fin_d,
    x, a1, qs, ks, vs, att, lse, hid, a2, gelu, gp, cot,
    w_q, w_o, w_u, w_d, g_q, g_d,
    bias_own, biases, bs_own, bs_buf, m_same, m_lt, m_le,
    turned, e1s, e1r, e2s, e2r, e3r, e4r, ybuf, hals, halr, halz, tg, dk, dv,
    *rest,
):
    sm, smr, smz, ub, qb, ss, rs, ls = rest[-8:]
    RA, RB, RC, RD = ({g: rest[4 * k + i] for k, (g, _, _) in enumerate(RED)} for i in range(4))
    R = tok_ref.shape[0]
    D = tok_ref.shape[1]
    w = lax.axis_index("wide")
    z = lax.axis_index("narrow")
    c = lax.rem(w, 2)
    xx = lax.rem(lax.div(w, 2), 2)
    yy = lax.rem(lax.div(w, 4), 2)
    t = lax.div(z, 2)
    h = lax.rem(z, 2)
    wc = w + 1 - 2 * c
    wx = w + 2 - 4 * xx
    wy = w + 4 - 8 * yy
    z1 = z + 1 - 2 * h
    z2 = z + 2 - 4 * t
    z3 = 3 - z
    entry = 2 - c
    far = 3 - 3 * c
    home = c == t
    away = jnp.logical_not(home)
    is_entry = z == entry
    is_far = z == far

    sends, recvs, locals_ = itertools.count(), itertools.count(), itertools.count()
    pending = []

    def take(counter, n=1):
        first = next(counter)
        for _ in range(n - 1):
            next(counter)
        return first

    def when(cond, fn):
        if cond is None:
            fn()
        else:
            @pl.when(cond)
            def _():
                fn()

    def remote(src, dst, si, ri, dev):
        return pltpu.make_async_remote_copy(
            src_ref=src, dst_ref=dst, send_sem=ss.at[si], recv_sem=rs.at[ri],
            device_id=dev, device_id_type=MESH,
        )

    most = x.shape[0]

    def send(src, dst, ri, dev, cond=None, group=pending):
        n = src.size * jnp.dtype(src.dtype).itemsize // (2 * D)
        for entry_ in group:
            if entry_[0] is cond and entry_[2] + n <= most:
                entry_[2] += n
                break
        else:
            entry_ = [cond, take(sends), n]
            group.append(entry_)
        cp = remote(src, dst, entry_[1], ri, dev)
        when(cond, lambda: cp.start())

    def sent(group):
        for cond, si, n in group:
            piece = x.at[pl.ds(0, n)]
            cp = remote(piece, piece, si, 0, (wc, z))
            when(cond, lambda: cp.wait_send())
        group.clear()

    def recv(dst, ri, cond=None):
        cp = remote(dst, dst, 0, ri, (wc, z))
        when(cond, lambda: cp.wait_recv())

    def local(src, dst, cond=None):
        cp = pltpu.make_async_copy(src, dst, ls.at[take(locals_)])
        when(cond, lambda: cp.start())
        return lambda: when(cond, lambda: cp.wait())

    def rows(start, n):
        return pl.ds(pl.multiple_of(start, 128), n)

    def loop(lo, hi, fn):
        def step(i, _):
            fn(i)
            return 0

        lax.fori_loop(lo, hi, step, 0)

    W, IN = {Q: w_q, O: w_o}, {Q: in_q, O: in_o}
    G, FIN = {O: w_o}, {O: fin_o}
    for k in range(2):
        half = pl.ds(k, 1)
        u, d = (U0, U1)[k], (D0, D1)[k]
        W[u], W[d] = w_u.at[half], w_d.at[half]
        IN[u], IN[d] = in_u.at[half], in_d.at[half]
        G[u], G[d] = w_u.at[half], g_d.at[half]
        FIN[u], FIN[d] = fin_u.at[half], fin_d.at[half]
    for p in range(3):
        G[Q0 + p] = g_q.at[:, p]
        FIN[Q0 + p] = fin_q.at[:, p]
    HC = 6 * HEAD_DIM
    NP = HC // 128
    NC = 2 * R // C
    HB = R // C

    barrier = pltpu.get_barrier_semaphore()
    wd = wx + 4 - 8 * yy
    plane = [(wc, z), (wx, z), (wy, z), (wd, z)]
    plane += [(v + 1 - 2 * c, z) for v in (wx, wy, wd)]
    partners = plane + [(w, z1), (w, z2), (w, z3), (wc, z2), (wc, z3)]
    for dev in partners:
        pl.semaphore_signal(barrier, inc=1, device_id=dev, device_id_type=MESH)
    pl.semaphore_wait(barrier, len(partners))

    w_native = {}
    w_sent = {g: [] for g, _, _ in GEO}
    wz_r = {g: take(recvs, 2) for g, _, _ in GEO}
    wxy_r = {g: take(recvs, 6) for g, _, _ in GEO}

    def weights_out(g, group=pending):
        src = IN[g].at[:, yy, xx]
        dst = W[g].at[:, h, yy, xx]
        send(src, dst, wz_r[g] + h, (w, entry), home, group)
        send(src, dst, wz_r[g] + h, (w, z1), home, group)

    def weights_native(g):
        w_native[g] = local(IN[g], W[g].at[:, h], home)

    foreign_ = [jnp.logical_not(jnp.logical_and(home, h == s)) for s in range(2)]

    def foreign(s):
        return foreign_[s]

    def weights_spread(g):
        for s in range(2):
            piece = W[g].at[:, s, yy, xx]
            recv(piece, wz_r[g] + s, foreign(s))
            relayed = 0 if s == 0 else 1
            for j, dev in enumerate((wx, wy)):
                r = wxy_r[g] + 3 * s + (0 if j == relayed else 2)
                send(piece, piece, r, (dev, z), foreign(s), w_sent[g])
            send(piece, piece, wz_r[g] + s, (w, far), is_entry, w_sent[g])

    def weights_relay(g):
        along_x = 0
        piece = W[g].at[:, along_x, yy, 1 - xx]
        r = wxy_r[g] + 3 * along_x
        recv(piece, r, foreign(along_x))
        send(piece, piece, r + 2, (wy, z), foreign(along_x), w_sent[g])
        along_y = 1 - along_x
        piece = W[g].at[:, along_y, 1 - yy, xx]
        r = wxy_r[g] + 3 * along_y
        recv(piece, r, foreign(along_y))
        send(piece, piece, r + 2, (wx, z), foreign(along_y), w_sent[g])

    def weights_wait(g):
        w_native[g]()
        along_x = 0
        along_y = 1 - along_x
        recv(W[g].at[:, along_x, 1 - yy], wxy_r[g] + 3 * along_x + 2, foreign(along_x))
        recv(W[g].at[:, along_y, :, 1 - xx], wxy_r[g] + 3 * along_y + 2, foreign(along_y))

    bs_own[...] = jnp.full(bs_own.shape, bs_ref[0], jnp.int32)
    bs_copy = remote(bs_own, bs_buf, take(sends), take(recvs), (wc, z))
    bs_copy.start()

    halves = [pl.ds(k * (R // 2), R // 2) for k in range(2)]

    def block(ref, b, k):
        return ref.at[pl.ds(pl.multiple_of(R * b + k * (R // 2), 128), R // 2)]

    tok_r = take(recvs, 6)
    tok_local = local(tok_ref, x.at[pl.ds(pl.multiple_of(R * c, 128), R)], home)
    slot = (1 - c) * (4 - z)
    zt = (1 - c) + c * (z + 2)
    halo_src = jnp.logical_and(c == 1, z == 2)
    def tokens_out(k):
        src = tok_ref.at[halves[k]]
        send(src, block(x, slot, k), tok_r + 2 * slot + k, (wc, zt), away)

    def tokens_home():
        for k in range(2):
            send(tok_ref.at[halves[k]], block(x, c, k), tok_r + 2 * c + k, (wc, z), home)
        for g, _, _ in GEO:
            weights_native(g)

    def halo_out(k):
        send(tok_ref.at[halves[k]], block(x, 2, k), tok_r + 4 + k, (w, 3), halo_src)

    params = (g1_ref, s1_ref, ob_ref, g2_ref, s2_ref, db_ref, upb_ref)

    def param(k):
        return params[k][...].astype(F32).reshape(1, D)

    bias_r = take(recvs, 2)
    bias_sent = []

    def place():
        row_i = lax.broadcasted_iota(jnp.int32, (HC // 2, HC), 0)
        col_i = lax.broadcasted_iota(jnp.int32, (HC // 2, HC), 1)
        source = lax.div(col_i, 128) * HEAD_DIM + lax.rem(col_i, HEAD_DIM)
        mine = lax.div(lax.rem(col_i, 128), HEAD_DIM) == h
        return jnp.logical_and(source == row_i, mine).astype(F32)

    def biases_out():
        bias_own[...] = jnp.zeros(bias_own.shape, F32)
        bias_own[0:3, 0:HC] = mm(qkvb_ref[...], place().astype(BF16))
        bias_own[3:4, pl.ds(pl.multiple_of(h * D, 128), D)] = param(6)
        for dz in (entry, z1, far):
            send(bias_own, biases.at[h], bias_r + h, (w, dz), home, bias_sent)

        @pl.when(home)
        def _():
            biases[h] = bias_own[...]

        @pl.when(h == 0)
        def _():
            x[pl.ds(2 * R, R), :] = jnp.zeros((R, D), BF16)

    gain1, shift1 = param(0), param(1)

    def norm_block(b):
        def step(i):
            r = rows(R * b + i * C, C)
            normed, _inv = norm_stats(x[r, :].astype(F32))
            a1[r, :] = (normed * gain1 + shift1).astype(BF16)

        loop(0, R // C, step)

    def masks():
        bs_copy.wait()
        pick = (t == c).astype(jnp.int32)
        bl = bs_own[0:1, :] * pick + bs_buf[0:1, :] * (1 - pick)
        bl = jnp.concatenate([bl, bl], axis=1)

        def block_of(v):
            return jnp.where(
                bl == 4,
                lax.shift_right_logical(v, 2),
                jnp.where(bl == 8, lax.shift_right_logical(v, 3), lax.shift_right_logical(v, 4)),
            )

        key_no = block_of(lax.broadcasted_iota(jnp.int32, (T, 2 * T), 0))
        row_no = block_of(lax.rem(lax.broadcasted_iota(jnp.int32, (T, 2 * T), 1), T))
        m_same[...] = jnp.where(key_no == row_no, 0.0, NEG)
        m_lt[...] = jnp.where(key_no < row_no, 0.0, NEG)
        m_le[...] = jnp.where(key_no <= row_no, 0.0, NEG)

    def norm_local():
        tok_local()
        for k in range(2):
            recv(block(x, 1 - c, k), tok_r + 2 * (1 - c) + k, away)
        norm_block(t)

    takes_halo = jnp.logical_and(c == 1, h == 1)
    feeds = jnp.logical_and(c == 1, z == 1)

    def halo_pass(k):
        recv(block(x, 2, k), tok_r + 4 + k, takes_halo)
        send(block(x, 2, k), block(x, 1, k), tok_r + 2 + k, (w, 0), feeds)
        send(block(x, 2, k), block(x, 2, k), tok_r + 4 + k, (wc, z), takes_halo)

    def tokens_pass(k):
        recv(block(x, c, k), tok_r + 2 * c + k, away)
        send(block(x, c, k), block(x, c, k), tok_r + 2 * c + k, (wc, z), away)

    cot_r = take(recvs, 4)
    cot_local = []

    def cotangents_out(k):
        src = cot_ref.at[halves[k]]
        send(src, block(cot, c, k), cot_r + 2 * c + k, (wc, z), home)
        send(src, block(cot, 1 - c, k), cot_r + 2 * (1 - c) + k, (wc, z2), away)
        cot_local.append(local(src, block(cot, c, k), home))

    def norm_other():
        for k in range(2):
            recv(block(x, 1 - c, k), tok_r + 2 * (1 - c) + k, home)
        norm_block(1 - t)

    def norm_halo():
        for k in range(2):
            recv(block(x, 2, k), tok_r + 4 + k, jnp.logical_and(c == 0, h == 1))
        norm_block(2)

    def biases_in():
        recv(biases.at[0], bias_r, foreign(0))
        recv(biases.at[1], bias_r + 1, foreign(1))
        sent(bias_sent)
        bias_own[...] = biases[0] + biases[1]


    def wq(j):
        return w_q[3 * j : 3 * j + 3].reshape(HC, D)

    def cos_sin(place, n):
        r = rows(place, n)
        return cos_ref[r, :], sin_ref[r, :]

    def project(i, halo):
        r = rows(i * C, C)
        a = a1[r, :]
        place = (i * C - 2 * R) if halo else (R * h + lax.rem(i * C, R))
        cs, sn = cos_sin(place, C)
        if not halo:
            qv = mm_nt(a, wq(0)) + bias_own[0:1, :HC]
            for p in range(NP):
                v = qv[:, p * 128 : p * 128 + 128]
                qs[p, r, :] = ((v * cs + swap_halves(v) * sn) * 0.125).astype(BF16)
        kv = mm_nt(a, wq(1)) + bias_own[1:2, :HC]
        for p in range(NP):
            v = kv[:, p * 128 : p * 128 + 128]
            ks[p, r, :] = (v * cs + swap_halves(v) * sn).astype(BF16)
        vv = mm_nt(a, wq(2)) + bias_own[2:3, :HC]
        for p in range(NP):
            vs[p, r, :] = vv[:, p * 128 : p * 128 + 128].astype(BF16)

    def project_block(b):
        loop(0, HB, lambda i: project(HB * b + i, False))

    def project_halo():
        loop(NC, NC + HB, lambda i: project(i, True))

    halo_bias = jnp.where(h == 1, 0.0, NEG).astype(F32)
    lane = lax.broadcasted_iota(jnp.int32, (1, 128), 1)
    lo_f = (lane < 64).astype(F32)
    lo_mask = lo_f.astype(BF16)
    hi_mask = (1.0 - lo_f).astype(BF16)

    def both_heads(v):
        return jnp.concatenate([v * lo_mask, v * hi_mask], axis=0)

    def one_of_each(v):
        return v[:T] * lo_f + v[T:] * (1.0 - lo_f)

    def key_parts(b, i):
        parts = []
        if b == 0:
            parts.append((T * i, T, m_same))
        if i > 0:
            parts.append((R, T * i, None))
        parts.append((R + T * i, T, m_lt if b == 0 else m_le))
        parts.append((2 * R, R, halo_bias))
        return parts

    def scores_of(p, part, qm):
        start, n, mask = part
        sc = mm_nt(ks[p, pl.ds(start, n), :], qm)
        return sc if mask is None or mask is halo_bias else sc + mask[...]

    def bias_of(part):
        return halo_bias if part[2] is halo_bias else 0.0

    chunks = [(b, i) for b in range(2) for i in range(R // T)]

    def attend(p, n):
        if n == 0:
            turned[...] = vs[p].T
        for b, i in chunks[n : n + 1]:
            r = pl.ds(R * b + T * i, T)
            qm = both_heads(qs[p, r, :])
            parts = key_parts(b, i)
            sc = [scores_of(p, part, qm) for part in parts]
            top = None
            for part, v in zip(parts, sc):
                m = jnp.max(v, axis=0, keepdims=True) + bias_of(part)
                top = m if top is None else jnp.maximum(top, m)
            total, out = None, None
            for part, v in zip(parts, sc):
                e = jnp.exp(v - (top - bias_of(part)))
                l = jnp.sum(e, axis=0, keepdims=True)
                o = mm(turned[:, pl.ds(part[0], part[1])], e.astype(BF16))
                total = l if total is None else total + l
                out = o if out is None else out + o
            out = out / total
            att[p, r, :] = one_of_each(out.T).astype(BF16)
            lse[p, n] = top + jnp.log(total)

    e1_r = take(recvs, 4)
    e1_s = take(sends, 4)
    def swap_out(i, dst, si, ri):
        r = rows(i * C, C)
        remote(e1s.at[r], dst.at[r], si + i, ri + i, (wc, z)).start()

    def swap_in(i, dst, ri):
        r = rows(i * C, C)
        remote(dst.at[r], dst.at[r], 0, ri + i, (wc, z)).wait_recv()

    def swap_done(i, dst, si):
        r = rows(i * C, C)
        remote(e1s.at[r], dst.at[r], si + i, 0, (wc, z)).wait_send()

    def pairs(ref, r):
        return jnp.concatenate([ref[p, r, :] for p in range(NP)], axis=1)

    def out_project(i):
        r = rows(i * C, C)
        e1s[r, :] = mm(pairs(att, r), w_o[...].reshape(HC, D)).astype(BF16)
        swap_out(i, e1r, e1_s, e1_r)


    def clear():
        sm[...] = jnp.zeros(sm.shape, F32)
        ub[...] = jnp.zeros(ub.shape, F32)
        qb[...] = jnp.zeros(qb.shape, F32)

    out_bias, gain2, shift2, down_bias = param(2), param(3), param(4), param(5)
    KG = float(np.sqrt(2.0 / np.pi))

    def wu(s):
        return jnp.concatenate([w_u[0, s].reshape(D // 2, D), w_u[1, s].reshape(D // 2, D)], axis=0)

    def wd(s):
        return jnp.concatenate([w_d[0, s].reshape(D // 2, D), w_d[1, s].reshape(D // 2, D)], axis=0)

    def feed(i):
        r = rows(i * C, C)
        swap_in(i, e1r, e1_r)
        hv = x[r, :].astype(F32) + e1s[r, :].astype(F32) + e1r[r, :].astype(F32) + out_bias
        hid[r, :] = hv
        normed, _inv = norm_stats(hv)
        act = (normed * gain2 + shift2).astype(BF16)
        a2[r, :] = act
        for s in range(2):
            cols = pl.ds(s * D, D)
            u = mm(act, wu(s)) + bias_own[3:4, s * D : (s + 1) * D]
            u2 = u * u
            th = jnp.tanh(KG * u * (1.0 + 0.044715 * u2))
            half = 0.5 * (1.0 + th)
            gelu[r, cols] = (u * half).astype(BF16)
            slope = half + 0.5 * u * (1.0 - th * th) * (KG * (1.0 + 3 * 0.044715 * u2))
            gp[r, cols] = slope.astype(BF16)

    def cot_pass(k):
        cot_local[k]()
        recv(block(cot, c, k), cot_r + 2 * c + k, away)
        send(block(cot, c, k), block(cot, c, k), cot_r + 2 * c + k, (wc, z), away)

    def cot_in():
        for k in range(2):
            recv(block(cot, 1 - c, k), cot_r + 2 * (1 - c) + k)

    ra_r = {g: take(recvs, 2) for g, _, _ in RED}
    rb_r = {g: take(recvs, 2) for g, _, _ in RED}
    rc_r = {g: take(recvs, 2) for g, _, _ in RED}
    rd_r = {g: take(recvs, 2) for g, _, _ in RED}
    fin_r = {g: take(recvs, 3) for g, _, _ in RED}
    pass_r = take(recvs, 2)
    fin_local = {}
    size = {g: (n, r) for g, n, r in RED}
    turn = {g: k % 2 for k, (g, _, _) in enumerate(RED)}

    def add(dst, src):
        dst[...] = (dst[...].astype(F32) + src[...].astype(F32)).astype(BF16)

    def reduce_a(g):
        send(G[g].at[:, 0, :, 1 - xx], RA[g].at[0], ra_r[g], (wx, z))
        send(G[g].at[:, 1, 1 - yy, :], RA[g].at[1], ra_r[g] + 1, (wy, z))

    def reduce_b(g):
        n, r = size[g]
        recv(RA[g].at[0], ra_r[g])
        for k in range(n):
            add(G[g].at[k, 0, 1 - yy, xx], RA[g].at[0, k, 1 - yy])
        send(G[g].at[:, 0, 1 - yy, xx], RB[g].at[0], rb_r[g], (wy, z))
        recv(RA[g].at[1], ra_r[g] + 1)
        for k in range(n):
            add(G[g].at[k, 1, yy, 1 - xx], RA[g].at[1, k, 1 - xx])
        send(G[g].at[:, 1, yy, 1 - xx], RB[g].at[1], rb_r[g] + 1, (wx, z))
        for k in range(n):
            add(G[g].at[k, 0, yy, xx], RA[g].at[0, k, yy])
            add(G[g].at[k, 1, yy, xx], RA[g].at[1, k, xx])

    def reduce_c(g):
        n, r = size[g]
        for s in range(2):
            recv(RB[g].at[s], rb_r[g] + s)
            for k in range(n):
                add(G[g].at[k, s, yy, xx], RB[g].at[s, k])
            piece = G[g].at[:, s, yy, xx]
            if g in DIRECT:
                at = (w, 2 * c + s)
                send(piece, RC[g].at[0], rc_r[g], at, is_far)
                send(piece, RD[g].at[1], rd_r[g] + 1, at, is_entry)
            else:
                send(piece, RC[g].at[s], rc_r[g] + s, (w, entry), is_far)
            send(piece, RD[g].at[0], rd_r[g], (w, z1), jnp.logical_and(home, h == 1 - s))

    def reduce_d(g):
        n, r = size[g]
        if g in DIRECT:
            return
        for s in range(2):
            recv(RC[g].at[s], rc_r[g] + s, is_entry)

            @pl.when(is_entry)
            def _():
                for k in range(n):
                    add(G[g].at[k, s, yy, xx], RC[g].at[s, k])

            send(G[g].at[:, s, yy, xx], RD[g].at[1], rd_r[g] + 1, (w, 2 * c + s), is_entry)

    def reduce_e(g):
        n, r = size[g]
        recv(RD[g].at[0], rd_r[g], home)
        recv(RD[g].at[1], rd_r[g] + 1, home)
        if g in DIRECT:
            recv(RC[g].at[0], rc_r[g], home)

        @pl.when(home)
        def _():
            for k in range(n):
                dst = G[g].at[k, h, yy, xx]
                v = dst[...].astype(F32) + RD[g][0, k].astype(F32) + RD[g][1, k].astype(F32)
                if g in DIRECT:
                    v = v + RC[g][0, k].astype(F32)
                dst[...] = v.astype(BF16)

        piece = G[g].at[:, h, yy, xx]
        out = FIN[g].at[:, yy, xx]
        fin_local[g] = local(piece, out, home)
        for j, dev in enumerate((wx, wy)):
            send(piece, out, fin_r[g] + j, (dev, z), home)
        send(piece, out, pass_r + int(g in (O, Q0, Q1, Q2)), (wc, z), home)

    def reduce_f(g):
        for j, (py, px) in enumerate(((yy, 1 - xx), (1 - yy, xx))):
            piece = FIN[g].at[:, py, px]
            recv(piece, fin_r[g] + j, home)
            if j == turn[g]:
                send(piece, piece, fin_r[g] + 2, ((wy, wx)[j], z), home)
            send(piece, piece, pass_r + int(g in (O, Q0, Q1, Q2)), (wc, z), home)

    def reduce_g(g):
        piece = FIN[g].at[:, 1 - yy, 1 - xx]
        recv(piece, fin_r[g] + 2, home)
        send(piece, piece, pass_r + int(g in (O, Q0, Q1, Q2)), (wc, z), home)

    def results_in():
        for g, _, _ in RED:
            fin_local[g]()
        for k, n in enumerate((2 * D, D)):
            recv(x.at[pl.ds(0, n)], pass_r + k, away)

    def grad_down(half, s):
        cols = pl.ds(pl.multiple_of(s * D + half * (D // 2), 128), D // 2)
        g = mm_tn(gelu[:, cols], cot[...])
        g_d[half, s] = g.astype(BF16).reshape(2, 2, 96, D)

    def grad_up(half, s):
        g = mm_tn(
            a2[:, half * (D // 2) : (half + 1) * (D // 2)],
            gp[:, pl.ds(pl.multiple_of(s * D, 128), D)],
        )
        w_u[half, s] = g.astype(BF16).reshape(2, 2, 96, D)

    def grads_down(half):
        loop(0, 2, lambda s: grad_down(half, s))

    def grads_up(half):
        sent(w_sent[U0 + half])
        loop(0, 2, lambda s: grad_up(half, s))

    e3_r, e3_s = take(recvs, 4), take(sends, 4)

    def back_up(i):
        r = rows(i * C, C)
        cv = cot[r, :]
        out = None
        for s in range(2):
            cols = pl.ds(s * D, D)
            gu = (mm_nt(cv, wd(s)) * gp[r, cols].astype(F32)).astype(BF16)
            gp[r, cols] = gu
            ub[0:1, cols] += jnp.sum(gu.astype(F32), axis=0, keepdims=True)
            o = mm_nt(gu, wu(s))
            out = o if out is None else out + o
        e1s[r, :] = out.astype(BF16)
        swap_out(i, e3r, e3_s, e3_r)

    def backs_up():
        loop(0, NC, lambda i: swap_done(i, e1r, e1_s))
        loop(0, NC, back_up)

    e2_r, e2_s = take(recvs, 2), take(sends, 2)

    def down_of(r):
        return mm(gelu[r, 0:D], wd(0)) + mm(gelu[r, D : 2 * D], wd(1))

    def down_other(i):
        r = rows(R * (1 - c) + i * C, C)
        d = rows(i * C, C)
        e2s[d, :] = down_of(r).astype(BF16)
        remote(e2s.at[d], e2r.at[d], e2_s + i, e2_r + i, (wc, z)).start()

    def down_own(i):
        r = rows(R * c + i * C, C)
        d = rows(i * C, C)
        part = down_of(r)
        remote(e2r.at[d], e2r.at[d], 0, e2_r + i, (wc, z)).wait_recv()
        y = hid[r, :] + part + e2r[d, :].astype(F32) + down_bias
        ybuf[d, :] = y.astype(BF16)
        sm[5:6, :] += jnp.sum(cot[r, :].astype(F32), axis=0, keepdims=True)

    z_orig = 2 * c + h
    y_r = take(recvs)
    y_local = []

    def down_mine():
        loop(0, HB, down_own)
        y_local.append(local(ybuf, act_out, home))
        send(ybuf, act_out, y_r, (wc, z_orig), away)

    def norm2_back(i):
        r = rows(i * C, C)
        swap_in(i, e3r, e3_r)
        g2 = e1s[r, :].astype(F32) + e3r[r, :].astype(F32)
        normed, inv = norm_stats(hid[r, :])
        gh = cot[r, :].astype(F32) + norm_back(g2, normed, inv, gain2)
        hid[r, :] = gh
        own = (lax.div(i, HB) == c).astype(F32)
        sm[3:4, :] += own * jnp.sum(g2 * normed, axis=0, keepdims=True)
        sm[4:5, :] += own * jnp.sum(g2, axis=0, keepdims=True)
        sm[2:3, :] += own * jnp.sum(gh, axis=0, keepdims=True)
        swap_done(i, e3r, e3_s)
        br = gh.astype(BF16)
        e1s[r, :] = br
        a2[r, 0:HC] = mm_nt(br, w_o[...].reshape(HC, D)).astype(BF16)

    def grad_out():
        everything = pl.ds(0, 2 * R)
        sent(w_sent[O])
        g_out = mm_tn(pairs(att, everything), e1s[...])
        w_o[...] = g_out.astype(BF16).reshape(3, 2, 2, 2, 16, D)

    def attend_back(p, n):
        if n == 0:
            dk[...] = jnp.zeros(dk.shape, F32)
            dv[...] = jnp.zeros(dv.shape, F32)
            turned[...] = ks[p].T
        for b, i in chunks[n : n + 1]:
            r = pl.ds(R * b + T * i, T)
            qm = both_heads(qs[p, r, :])
            ga = a2[r, p * 128 : p * 128 + 128]
            gm = both_heads(ga)
            parts = key_parts(b, i)
            log_total = lse[p, n]
            inner = (ga.astype(F32) * att[p, r, :].astype(F32)).T
            delta = jnp.concatenate(
                [
                    jnp.sum(inner[:HEAD_DIM], axis=0, keepdims=True),
                    jnp.sum(inner[HEAD_DIM:], axis=0, keepdims=True),
                ],
                axis=1,
            )
            dq = None
            for part in parts:
                k = pl.ds(part[0], part[1])
                pr = jnp.exp(scores_of(p, part, qm) - (log_total - bias_of(part)))
                ds = (pr * (mm_nt(vs[p, k, :], gm) - delta)).astype(BF16)
                dv[k, :] += mm(pr.astype(BF16), gm)
                dk[k, :] += mm(ds, qm)
                d = mm(turned[:, k], ds)
                dq = d if dq is None else dq + d
            dq = one_of_each(dq.T) * 0.125
            cs, sn = cos_sin(R * h + T * i, T)
            dq = (dq * cs - swap_halves(dq) * sn).astype(BF16)
            qs[p, r, :] = dq

    def attend_end(p):
        for b in range(3):
            cs, sn = cos_sin(R * h if b < 2 else 0, R)
            r = pl.ds(R * b, R)
            v = dk[r, :]
            ks[p, r, :] = (v * cs - swap_halves(v) * sn).astype(BF16)
            vs[p, r, :] = dv[r, :].astype(BF16)

    def grad_qkv(p):
        r, o = pl.ds(0, 2 * R), pl.ds(2 * R, R)
        lhs = jnp.concatenate([qs[p, r, :], ks[p, r, :], vs[p, r, :]], axis=1)
        over = jnp.concatenate([ks[p, o, :], vs[p, o, :]], axis=1)
        g = mm_tn(lhs, a1[r, :])
        g_over = mm_tn(over, a1[o, :])
        g_q[0, p] = g[:128].astype(BF16).reshape(2, 2, 2, 16, D)
        for j in range(2):
            part = g[128 * (j + 1) : 128 * (j + 2)] + g_over[128 * j : 128 * (j + 1)]
            g_q[j + 1, p] = part.astype(BF16).reshape(2, 2, 2, 16, D)
        cols = pl.ds(128 * p, 128)
        qb[0:1, cols] = jnp.sum(qs[p, r, :].astype(F32), axis=0, keepdims=True)
        qb[1:2, cols] = jnp.sum(ks[p].astype(F32), axis=0, keepdims=True)
        qb[2:3, cols] = jnp.sum(vs[p].astype(F32), axis=0, keepdims=True)

    def back_qkv(r, halo):
        g = mm(pairs(ks, r), wq(1)) + mm(pairs(vs, r), wq(2))
        return g if halo else g + mm(pairs(qs, r), wq(0))

    hal_r, hal_s = take(recvs, 2), take(sends, 2)
    halz_r = take(recvs, 2)
    e4_r, e4_s = take(recvs, 2), take(sends, 2)

    def halo_back(i):
        d = rows(i * C, C)
        hals[d, :] = back_qkv(rows(2 * R + i * C, C), True).astype(BF16)

        @pl.when(c == 0)
        def _():
            remote(hals.at[d], halr.at[d], hal_s + i, hal_r + i, (wc, z)).start()

    def halos_back():
        loop(0, HB, halo_back)

    def other_back(i):
        d = rows(i * C, C)
        e2s[d, :] = back_qkv(rows(R * (1 - c) + i * C, C), False).astype(BF16)
        remote(e2s.at[d], e4r.at[d], e4_s + i, e4_r + i, (wc, z)).start()

    def others_back():
        loop(0, HB, lambda i: remote(
            e2s.at[rows(i * C, C)], e2r.at[rows(i * C, C)], e2_s + i, 0, (wc, z)).wait_send())
        loop(0, HB, other_back)

    def halo_sum(k):
        d = pl.ds(k * C, C)
        recv(halr.at[d], hal_r + k, c == 1)

        @pl.when(c == 1)
        def _():
            add(hals.at[d], halr.at[d])

        send(hals.at[d], halz.at[d], halz_r + k, (w, z1), jnp.logical_and(c == 1, h == 1))

    def own_back(i):
        tg[rows(i * C, C), :] = back_qkv(rows(R * c + i * C, C), False)

    def owns_back():
        loop(0, HB, own_back)

        @pl.when(jnp.logical_not(gets))
        def _():
            halz[...] = jnp.zeros(halz.shape, BF16)

    gets = jnp.logical_and(c == 1, h == 0)
    t_r = take(recvs, 2)

    def norm1_back(i):
        d = pl.ds(i * C, C)
        r = rows(R * c + i * C, C)
        recv(halz.at[d], halz_r + i, gets)
        remote(e4r.at[d], e4r.at[d], 0, e4_r + i, (wc, z)).wait_recv()
        g1 = tg[d, :] + e4r[d, :].astype(F32) + halz[d, :].astype(F32)
        normed, inv = norm_stats(x[r, :].astype(F32))
        out = hid[r, :] + norm_back(g1, normed, inv, gain1)
        sm[0:1, :] += jnp.sum(g1 * normed, axis=0, keepdims=True)
        sm[1:2, :] += jnp.sum(g1, axis=0, keepdims=True)
        e1r[d, :] = out.astype(BF16)
        send(e1r.at[d], tgrad_out.at[d], t_r + i, (wc, z_orig), away)
        t_local.append(local(e1r.at[d], tgrad_out.at[d], home))

    t_local = []

    me = lax.rem(w, 8)
    base = w - me
    sm_r, sm2_r = take(recvs, 8), take(recvs, 4)

    def small_out_plane():
        cf = c.astype(F32)
        for j in range(3):
            sm[6 + j : 7 + j, 0:HC] = qb[j : j + 1, :] * (1.0 - cf)
            sm[6 + j : 7 + j, HC : 2 * HC] = qb[j : j + 1, :] * cf
        for s in range(2):
            sm[9 + s : 10 + s, :] = ub[0:1, s * D : (s + 1) * D] * (1.0 - cf)
            sm[11 + s : 12 + s, :] = ub[0:1, s * D : (s + 1) * D] * cf
        smr[me] = sm[...]
        for dev in plane:
            send(smr.at[me], smr.at[me], sm_r + me, dev)

    def small_out_z():
        for dev, _ in plane:
            other = dev - base
            recv(smr.at[other], sm_r + other)
        total = smr[0]
        for k in range(1, 8):
            total = total + smr[k]
        smz[z] = total
        for dev in (z1, z2, z3):
            send(smz.at[z], smz.at[z], sm2_r + z, (w, dev))

    def small_end():
        for dev in (z1, z2, z3):
            recv(smz.at[dev], sm2_r + dev)
        total = smz[0] + smz[1] + smz[2] + smz[3]
        sm[...] = total
        small_out[...] = total
        small_out[9:10, :] = sm[pl.ds(9 + z, 1), :]
        mine = sm[6:9, pl.ds(pl.multiple_of(HC * t, 128), HC)]
        small_out[6:9, 0 : HC // 2] = lax.dot_general(
            mine, place(), (((1,), (1,)), ((), ())), precision=lax.Precision.HIGHEST,
            preferred_element_type=F32,
        )

    weights_out(Q)
    biases_out()
    halo_out(0)
    tokens_out(0)
    halo_out(1)
    weights_spread(Q)
    halo_pass(0)
    tokens_out(1)
    tokens_pass(0)
    weights_out(O)
    tokens_home()
    weights_relay(Q)
    norm_local()
    weights_spread(O)
    masks()
    halo_pass(1)
    weights_out(U0)
    tokens_pass(1)
    weights_relay(O)
    weights_spread(U0)
    norm_halo()
    biases_in()
    weights_wait(Q)
    weights_out(U1)
    project_block(t)
    norm_other()
    weights_out(D0)
    project_block(1 - t)
    weights_spread(U1)
    project_halo()
    attend(0, 0)
    attend(0, 1)
    clear()
    cotangents_out(0)
    weights_wait(O)
    attend(0, 2)
    attend(0, 3)
    attend(0, 4)
    attend(0, 5)
    weights_relay(U0)
    attend(0, 6)
    weights_out(D1)
    attend(0, 7)
    attend(1, 0)
    attend(1, 1)
    attend(1, 2)
    attend(1, 3)
    weights_relay(U1)
    weights_spread(D0)
    attend(1, 4)
    attend(1, 5)
    attend(1, 6)
    attend(1, 7)
    attend(2, 0)
    attend(2, 1)
    attend(2, 2)
    cotangents_out(1)
    attend(2, 3)
    weights_wait(U0)
    attend(2, 4)
    attend(2, 5)
    attend(2, 6)
    weights_spread(D1)
    attend(2, 7)
    loop(0, NC, out_project)
    weights_relay(D0)
    weights_wait(U1)
    loop(0, NC, feed)
    weights_relay(D1)
    cot_pass(0)
    cot_pass(1)
    weights_wait(D0)
    cot_in()
    grads_down(0)
    weights_wait(D1)
    reduce_a(D0)
    loop(0, HB, down_other)
    grads_down(1)
    reduce_a(D1)
    backs_up()
    reduce_b(D0)
    grads_up(0)
    reduce_a(U0)
    down_mine()
    grads_up(1)
    loop(0, NC, norm2_back)
    attend_back(0, 0)
    reduce_a(U1)
    attend_back(0, 1)
    reduce_b(D1)
    attend_back(0, 2)
    attend_back(0, 3)
    attend_back(0, 4)
    attend_back(0, 5)
    reduce_c(D0)
    reduce_b(U0)
    attend_back(0, 6)
    attend_back(0, 7)
    attend_end(0)
    grad_out()
    attend_back(1, 0)
    reduce_a(O)
    attend_back(1, 1)
    reduce_c(D1)
    grad_qkv(0)
    attend_back(1, 2)
    attend_back(1, 3)
    attend_back(1, 4)
    reduce_b(U1)
    attend_back(1, 5)
    attend_back(1, 6)
    attend_back(1, 7)
    attend_end(1)
    attend_back(2, 0)
    reduce_b(O)
    reduce_d(D0)
    attend_back(2, 1)
    reduce_a(Q0)
    reduce_c(U1)
    attend_back(2, 2)
    grad_qkv(1)
    reduce_a(Q1)
    reduce_c(O)
    reduce_d(D1)
    attend_back(2, 3)
    reduce_e(D0)
    reduce_c(U0)
    attend_back(2, 4)
    attend_back(2, 5)
    attend_back(2, 6)
    attend_back(2, 7)
    attend_end(2)
    reduce_b(Q1)
    reduce_d(U1)
    reduce_b(Q0)
    halos_back()
    halo_sum(0)
    grad_qkv(2)
    reduce_e(U1)
    reduce_e(O)
    reduce_c(Q0)
    reduce_e(D1)
    halo_sum(1)
    reduce_a(Q2)
    reduce_c(Q1)
    reduce_f(O)
    others_back()
    reduce_d(U0)
    reduce_f(D0)
    reduce_b(Q2)
    reduce_e(Q0)
    reduce_g(D0)
    reduce_e(U0)
    reduce_e(Q1)
    owns_back()
    reduce_c(Q2)
    reduce_f(Q0)
    norm1_back(0)
    reduce_e(Q2)
    norm1_back(1)
    small_out_plane()
    reduce_f(Q1)
    reduce_f(Q2)
    reduce_g(O)
    reduce_g(Q0)
    reduce_g(Q2)
    reduce_f(D1)
    small_out_z()
    reduce_g(Q1)
    reduce_f(U0)
    reduce_f(U1)
    reduce_g(U0)
    reduce_g(D1)
    reduce_g(U1)
    small_end()
    results_in()
    recv(act_out, y_r, away)
    y_local[0]()
    for k in range(HB):
        d = pl.ds(k * C, C)
        recv(tgrad_out.at[d], t_r + k, away)
        t_local[k]()
    loop(0, HB, lambda i: remote(
        e2s.at[rows(i * C, C)], e4r.at[rows(i * C, C)], e4_s + i, 0, (wc, z)).wait_send())

    @pl.when(c == 0)
    def _():
        for k in range(HB):
            d = pl.ds(k * C, C)
            remote(hals.at[d], halr.at[d], hal_s + k, 0, (wc, z)).wait_send()

    sent(w_sent[Q])
    sent(w_sent[D0])
    sent(w_sent[D1])
    sent(pending)
    counts = (next(sends), next(recvs), next(locals_))
    assert counts[0] <= ss.shape[0] and counts[1] <= rs.shape[0] and counts[2] <= ls.shape[0], counts


def finish_kernel(
    small_ref, q_ref, o_ref, u_ref, d_ref, act_ref, tg_ref,
    g1, s1, ob, g2, s2, db, upb, qkvb, gq, go, gu, gd, act, tg,
    low, high, kept, ls, ss, cs,
):
    n = low.shape[1]
    parts = [
        (src.at[pl.ds(k, n)], dst.at[pl.ds(k, n)])
        for src, dst in ((u_ref, gu), (d_ref, gd), (o_ref, go), (q_ref, gq))
        for k in range(0, src.shape[0], n)
    ]
    loads = [pltpu.make_async_copy(a, low.at[k], ls.at[k]) for k, (a, _) in enumerate(parts)]
    stores = [pltpu.make_async_copy(high.at[k], b, ss.at[k]) for k, (_, b) in enumerate(parts)]
    inward = [pltpu.make_async_copy(a, kept.at[k], cs.at[k]) for k, a in enumerate((act_ref, tg_ref))]
    outward = [pltpu.make_async_copy(kept.at[k], b, cs.at[2 + k]) for k, b in enumerate((act, tg))]
    for load in loads + inward:
        load.start()
    for k, out in enumerate((g1, s1, ob, g2, s2, db)):
        out[...] = small_ref[k, :]
    upb[...] = small_ref[9, :]
    qkvb[...] = small_ref[6:9, : qkvb.shape[1]]
    for k, load in enumerate(loads):
        load.wait()
        high[k] = low[k].astype(F32)
        stores[k].start()
    for load, store in zip(inward, outward):
        load.wait()
        store.start()
    for copy in stores + outward:
        copy.wait()


def finish(small, fq, fo, fu, fd, act, tgrad):
    n, D = fo.shape
    steps = (fq.shape[0] + fo.shape[0] + fu.shape[0] + fd.shape[0]) // n
    anyspec = pl.BlockSpec(memory_space=pl.ANY)
    vspec = pl.BlockSpec(memory_space=pltpu.VMEM)
    sds = jax.ShapeDtypeStruct
    return pl.pallas_call(
        finish_kernel,
        out_shape=[sds((D,), F32)] * 7 + [sds((3, n), F32)]
        + [sds(v.shape, F32) for v in (fq, fo, fu, fd)]
        + [sds(v.shape, v.dtype) for v in (act, tgrad)],
        in_specs=[vspec] + [anyspec] * 6,
        out_specs=[vspec] * 8 + [anyspec] * 6,
        scratch_shapes=[
            pltpu.VMEM((steps, n, D), BF16),
            pltpu.VMEM((steps, n, D), F32),
            pltpu.VMEM((2, *act.shape), BF16),
            pltpu.SemaphoreType.DMA((steps,)),
            pltpu.SemaphoreType.DMA((steps,)),
            pltpu.SemaphoreType.DMA((4,)),
        ],
        compiler_params=pltpu.CompilerParams(vmem_limit_bytes=61 * 1024 * 1024),
        name="finish",
    )(small, fq, fo, fu, fd, act, tgrad)


def shards(
    tokens, block_size, ln1_gain, ln1_shift, qkv_weight, qkv_bias, out_weight, out_bias,
    ln2_gain, ln2_shift, up_weight, up_bias, down_weight, down_bias, cotangent, groups,
):
    R, D = tokens.shape
    local_width = qkv_weight.shape[2]
    HC = 2 * local_width
    FC = 2 * up_weight.shape[1]
    cos, sin = tables(2 * R)
    wq = jnp.transpose(qkv_weight, (1, 2, 0)).reshape(9, 2, 2, 16, D)
    wo = out_weight.reshape(3, 2, 2, 16, D)
    wu = up_weight.reshape(2, 2, 2, 96, D)
    wdn = down_weight.reshape(2, 2, 2, 96, D)
    anyspec = pl.BlockSpec(memory_space=pl.ANY)
    vspec = pl.BlockSpec(memory_space=pltpu.VMEM)
    sds = jax.ShapeDtypeStruct
    fins = [sds((3, 3, 2, 2, 16, D), BF16), sds((3, 2, 2, 16, D), BF16)]
    fins += [sds((2, 2, 2, 96, D), BF16)] * 2
    V = pltpu.VMEM
    weights = [V((n, 2, 2, 2, r, D), BF16) for n, r in ((9, 16), (3, 16), (2, 96), (2, 96))]
    recvs = []
    for _, n, r in RED:
        recvs += [
            V((2, n, 2, r, D), BF16),
            V((2, n, r, D), BF16),
            V((2, n, r, D), BF16),
            V((2, n, r, D), BF16),
        ]
    NP = HC // 128
    outs = pl.pallas_call(
        layer_kernel,
        out_shape=[sds((R, D), BF16), sds((R, D), BF16), sds((16, D), F32)] + fins,
        in_specs=[vspec] * 10 + [pl.BlockSpec(memory_space=pltpu.SMEM)] + [anyspec] * 6,
        out_specs=[anyspec, anyspec, vspec] + [anyspec] * 4,
        scratch_shapes=[
            V((3 * R, D), BF16),
            V((3 * R, D), BF16),
            V((NP, 2 * R, 128), BF16),
            V((NP, 3 * R, 128), BF16),
            V((NP, 3 * R, 128), BF16),
            V((NP, 2 * R, 128), BF16),
            V((NP, 2 * R // T, 1, 2 * T), F32),
            V((2 * R, D), F32),
            V((2 * R, D), BF16),
            V((2 * R, FC), BF16),
            V((2 * R, FC), BF16),
            V((2 * R, D), BF16),
            *weights,
            V((3, 3, 2, 2, 2, 16, D), BF16),
            V((2, 2, 2, 2, 96, D), BF16),
            V((8, FC), F32),
            V((2, 8, FC), F32),
            V((8, 128), jnp.int32),
            V((8, 128), jnp.int32),
            V((T, 2 * T), F32),
            V((T, 2 * T), F32),
            V((T, 2 * T), F32),
            V((128, 3 * R), BF16),
            V((2 * R, D), BF16),
            V((2 * R, D), BF16),
            V((R, D), BF16),
            V((R, D), BF16),
            V((2 * R, D), BF16),
            V((R, D), BF16),
            V((R, D), BF16),
            V((R, D), BF16),
            V((R, D), BF16),
            V((R, D), BF16),
            V((R, D), F32),
            V((3 * R, 128), F32),
            V((3 * R, 128), F32),
            *recvs,
            V((16, D), F32),
            V((8, 16, D), F32),
            V((4, 16, D), F32),
            V((8, FC), F32),
            V((8, HC), F32),
            pltpu.SemaphoreType.DMA((260,)),
            pltpu.SemaphoreType.DMA((220,)),
            pltpu.SemaphoreType.DMA((24,)),
        ],
        compiler_params=pltpu.CompilerParams(
            collective_id=0, has_side_effects=True, vmem_limit_bytes=62 * 1024 * 1024
        ),
        name="layer",
    )(
        jnp.asarray(cos), jnp.asarray(sin), ln1_gain, ln1_shift, out_bias, ln2_gain, ln2_shift,
        down_bias, up_bias, qkv_bias, block_size, tokens, cotangent, wq, wo, wu, wdn,
    )
    act, tgrad, small, fq, fo, fu, fd = outs
    if groups > 1:
        ids = [[g * 8 + k for g in range(groups)] for k in range(8)]
        small = lax.psum(small, "wide", axis_index_groups=ids)
    g1, s1, ob, g2, s2, db, upb, qkvb, gq, go, gu, gd, act, tgrad = finish(
        small, fq.reshape(3 * local_width, D), fo.reshape(local_width, D), fu.reshape(D, D),
        fd.reshape(D, D), act, tgrad,
    )
    if groups > 1:
        gq, go, gu, gd = lax.psum((gq, go, gu, gd), "wide", axis_index_groups=ids)
    gq = jnp.transpose(gq.reshape(3, local_width, D), (2, 0, 1))
    return act, tgrad, g1, s1, gq, qkvb, go, ob, g2, s2, gu, upb, gd, db


def solution(mesh):
    both = P(("wide", "narrow"), None)
    in_specs = (
        both, P("wide"), P(), P(), P(None, None, "narrow"), P(None, "narrow"), P("narrow", None), P(),
        P(), P(), P(None, "narrow"), P("narrow"), P("narrow", None), P(), both,
    )
    out_specs = (
        both, both, P(), P(), P(None, None, "narrow"), P(None, "narrow"), P("narrow", None), P(),
        P(), P(), P(None, "narrow"), P("narrow"), P("narrow", None), P(),
    )
    groups = mesh.shape["wide"] // 8

    def body(*args):
        return shards(*args, groups)

    return jax.shard_map(body, mesh=mesh, in_specs=in_specs, out_specs=out_specs, check_vma=False)
```

```python
import itertools

import jax
import jax.numpy as jnp
import numpy as np
from jax import lax
from jax.experimental import pallas as pl
from jax.experimental.pallas import tpu as pltpu
from jax.sharding import PartitionSpec as P

HEAD_DIM = 64
MESH = pl.DeviceIdType.MESH
F32 = jnp.float32
BF16 = jnp.bfloat16
NEG = -1e30
EPS = 1e-05
T = 128
C = 256
Q, O, U0, U1, D0, D1, Q0, Q1, Q2 = range(9)
GEO = ((Q, 9, 16), (O, 3, 16), (U0, 1, 96), (U1, 1, 96), (D0, 1, 96), (D1, 1, 96))
RED = (
    (D0, 1, 96), (D1, 1, 96), (U0, 1, 96), (U1, 1, 96),
    (O, 3, 16), (Q0, 3, 16), (Q1, 3, 16), (Q2, 3, 16),
)
DIRECT = (O, Q0, Q1, Q2)


def mm(a, b):
    return lax.dot_general(a, b, (((1,), (0,)), ((), ())), preferred_element_type=F32)


def mm_nt(a, b):
    return lax.dot_general(a, b, (((1,), (1,)), ((), ())), preferred_element_type=F32)


def mm_tn(a, b):
    return lax.dot_general(a, b, (((0,), (0,)), ((), ())), preferred_element_type=F32)


def norm_stats(v):
    mean = jnp.mean(v, axis=-1, keepdims=True)
    cen = v - mean
    inv = lax.rsqrt(jnp.mean(cen * cen, axis=-1, keepdims=True) + EPS)
    return cen * inv, inv


def norm_back(grad, normed, inv, gain):
    g = grad * gain
    return inv * (
        g
        - jnp.mean(g, axis=-1, keepdims=True)
        - normed * jnp.mean(g * normed, axis=-1, keepdims=True)
    )


def swap_halves(v):
    lane = lax.broadcasted_iota(jnp.int32, v.shape, 1)
    low = lax.rem(lane, 64) < 32
    return jnp.where(low, pltpu.roll(v, 96, 1), pltpu.roll(v, 32, 1))


def tables(half_len):
    freqs = np.exp(
        np.arange(HEAD_DIM // 2, dtype=np.float32)
        * np.float32(-2.0 * np.log(10000.0) / HEAD_DIM)
    ).astype(np.float32)
    angles = np.arange(half_len, dtype=np.float32)[:, None] * freqs[None, :]
    angles = angles.astype(np.float32)
    cos, sin = np.cos(angles), np.sin(angles)
    return (
        np.concatenate([cos, cos, cos, cos], 1).astype(np.float32),
        np.concatenate([-sin, sin, -sin, sin], 1).astype(np.float32),
    )


def layer_kernel(
    cos_ref, sin_ref, g1_ref, s1_ref, ob_ref, g2_ref, s2_ref, db_ref, upb_ref, qkvb_ref, bs_ref,
    tok_ref, cot_ref, in_q, in_o, in_u, in_d,
    act_out, tgrad_out, small_out, fin_q, fin_o, fin_u, fin_d,
    x, a1, qs, ks, vs, att, lse, hid, a2, gelu, gp, cot,
    w_q, w_o, w_u, w_d, g_q, g_d,
    bias_own, biases, bs_own, bs_buf, m_same, m_lt, m_le,
    turned, e1s, e1r, e2s, e2r, e3r, e4r, ybuf, hals, halr, halz, tg, dk, dv,
    *rest,
):
    sm, smr, smz, ub, qb, ss, rs, ls = rest[-8:]
    RA, RB, RC, RD = ({g: rest[4 * k + i] for k, (g, _, _) in enumerate(RED)} for i in range(4))
    R = tok_ref.shape[0]
    D = tok_ref.shape[1]
    w = lax.axis_index("wide")
    z = lax.axis_index("narrow")
    c = lax.rem(w, 2)
    xx = lax.rem(lax.div(w, 2), 2)
    yy = lax.rem(lax.div(w, 4), 2)
    t = lax.div(z, 2)
    h = lax.rem(z, 2)
    wc = w + 1 - 2 * c
    wx = w + 2 - 4 * xx
    wy = w + 4 - 8 * yy
    z1 = z + 1 - 2 * h
    z2 = z + 2 - 4 * t
    z3 = 3 - z
    entry = 2 - c
    far = 3 - 3 * c
    home = c == t
    away = jnp.logical_not(home)
    is_entry = z == entry
    is_far = z == far

    sends, recvs, locals_ = itertools.count(), itertools.count(), itertools.count()
    pending = []

    def take(counter, n=1):
        first = next(counter)
        for _ in range(n - 1):
            next(counter)
        return first

    def when(cond, fn):
        if cond is None:
            fn()
        else:
            @pl.when(cond)
            def _():
                fn()

    def remote(src, dst, si, ri, dev):
        return pltpu.make_async_remote_copy(
            src_ref=src, dst_ref=dst, send_sem=ss.at[si], recv_sem=rs.at[ri],
            device_id=dev, device_id_type=MESH,
        )

    most = x.shape[0]

    def send(src, dst, ri, dev, cond=None, group=pending):
        n = src.size * jnp.dtype(src.dtype).itemsize // (2 * D)
        for entry_ in group:
            if entry_[0] is cond and entry_[2] + n <= most:
                entry_[2] += n
                break
        else:
            entry_ = [cond, take(sends), n]
            group.append(entry_)
        cp = remote(src, dst, entry_[1], ri, dev)
        when(cond, lambda: cp.start())

    def sent(group):
        for cond, si, n in group:
            piece = x.at[pl.ds(0, n)]
            cp = remote(piece, piece, si, 0, (wc, z))
            when(cond, lambda: cp.wait_send())
        group.clear()

    def recv(dst, ri, cond=None):
        cp = remote(dst, dst, 0, ri, (wc, z))
        when(cond, lambda: cp.wait_recv())

    def local(src, dst, cond=None):
        cp = pltpu.make_async_copy(src, dst, ls.at[take(locals_)])
        when(cond, lambda: cp.start())
        return lambda: when(cond, lambda: cp.wait())

    def rows(start, n):
        return pl.ds(pl.multiple_of(start, 128), n)

    def loop(lo, hi, fn):
        def step(i, _):
            fn(i)
            return 0

        lax.fori_loop(lo, hi, step, 0)

    W, IN = {Q: w_q, O: w_o}, {Q: in_q, O: in_o}
    G, FIN = {O: w_o}, {O: fin_o}
    for k in range(2):
        half = pl.ds(k, 1)
        u, d = (U0, U1)[k], (D0, D1)[k]
        W[u], W[d] = w_u.at[half], w_d.at[half]
        IN[u], IN[d] = in_u.at[half], in_d.at[half]
        G[u], G[d] = w_u.at[half], g_d.at[half]
        FIN[u], FIN[d] = fin_u.at[half], fin_d.at[half]
    for p in range(3):
        G[Q0 + p] = g_q.at[:, p]
        FIN[Q0 + p] = fin_q.at[:, p]
    HC = 6 * HEAD_DIM
    NP = HC // 128
    NC = 2 * R // C
    HB = R // C

    barrier = pltpu.get_barrier_semaphore()
    wd = wx + 4 - 8 * yy
    plane = [(wc, z), (wx, z), (wy, z), (wd, z)]
    plane += [(v + 1 - 2 * c, z) for v in (wx, wy, wd)]
    partners = plane + [(w, z1), (w, z2), (w, z3), (wc, z2), (wc, z3)]
    for dev in partners:
        pl.semaphore_signal(barrier, inc=1, device_id=dev, device_id_type=MESH)
    pl.semaphore_wait(barrier, len(partners))

    w_native = {}
    w_sent = {g: [] for g, _, _ in GEO}
    wz_r = {g: take(recvs, 2) for g, _, _ in GEO}
    wxy_r = {g: take(recvs, 6) for g, _, _ in GEO}

    def weights_out(g, group=pending):
        src = IN[g].at[:, yy, xx]
        dst = W[g].at[:, h, yy, xx]
        send(src, dst, wz_r[g] + h, (w, entry), home, group)
        send(src, dst, wz_r[g] + h, (w, z1), home, group)

    def weights_native(g):
        w_native[g] = local(IN[g], W[g].at[:, h], home)

    foreign_ = [jnp.logical_not(jnp.logical_and(home, h == s)) for s in range(2)]

    def foreign(s):
        return foreign_[s]

    def weights_spread(g):
        for s in range(2):
            piece = W[g].at[:, s, yy, xx]
            recv(piece, wz_r[g] + s, foreign(s))
            relayed = 0 if s == int(g in (O, U1, D1)) else 1
            for j, dev in enumerate((wx, wy)):
                r = wxy_r[g] + 3 * s + (0 if j == relayed else 2)
                send(piece, piece, r, (dev, z), foreign(s), w_sent[g])
            send(piece, piece, wz_r[g] + s, (w, far), is_entry, w_sent[g])

    def weights_relay(g):
        along_x = int(g in (O, U1, D1))
        piece = W[g].at[:, along_x, yy, 1 - xx]
        r = wxy_r[g] + 3 * along_x
        recv(piece, r, foreign(along_x))
        send(piece, piece, r + 2, (wy, z), foreign(along_x), w_sent[g])
        along_y = 1 - along_x
        piece = W[g].at[:, along_y, 1 - yy, xx]
        r = wxy_r[g] + 3 * along_y
        recv(piece, r, foreign(along_y))
        send(piece, piece, r + 2, (wx, z), foreign(along_y), w_sent[g])

    def weights_wait(g):
        w_native[g]()
        along_x = int(g in (O, U1, D1))
        along_y = 1 - along_x
        recv(W[g].at[:, along_x, 1 - yy], wxy_r[g] + 3 * along_x + 2, foreign(along_x))
        recv(W[g].at[:, along_y, :, 1 - xx], wxy_r[g] + 3 * along_y + 2, foreign(along_y))

    bs_own[...] = jnp.full(bs_own.shape, bs_ref[0], jnp.int32)
    bs_copy = remote(bs_own, bs_buf, take(sends), take(recvs), (wc, z))
    bs_copy.start()

    halves = [pl.ds(k * (R // 2), R // 2) for k in range(2)]

    def block(ref, b, k):
        return ref.at[pl.ds(pl.multiple_of(R * b + k * (R // 2), 128), R // 2)]

    tok_r = take(recvs, 6)
    tok_local = local(tok_ref, x.at[pl.ds(pl.multiple_of(R * c, 128), R)], home)
    slot = (1 - c) * (4 - z)
    zt = (1 - c) + c * (z + 2)
    halo_src = jnp.logical_and(c == 1, z == 2)
    def tokens_out(k):
        src = tok_ref.at[halves[k]]
        send(src, block(x, slot, k), tok_r + 2 * slot + k, (wc, zt), away)

    def tokens_home():
        for k in range(2):
            send(tok_ref.at[halves[k]], block(x, c, k), tok_r + 2 * c + k, (wc, z), home)
        for g, _, _ in GEO:
            weights_native(g)

    def halo_out(k):
        send(tok_ref.at[halves[k]], block(x, 2, k), tok_r + 4 + k, (w, 3), halo_src)

    params = (g1_ref, s1_ref, ob_ref, g2_ref, s2_ref, db_ref, upb_ref)

    def param(k):
        return params[k][...].astype(F32).reshape(1, D)

    bias_r = take(recvs, 2)
    bias_sent = []

    def place():
        row_i = lax.broadcasted_iota(jnp.int32, (HC // 2, HC), 0)
        col_i = lax.broadcasted_iota(jnp.int32, (HC // 2, HC), 1)
        source = lax.div(col_i, 128) * HEAD_DIM + lax.rem(col_i, HEAD_DIM)
        mine = lax.div(lax.rem(col_i, 128), HEAD_DIM) == h
        return jnp.logical_and(source == row_i, mine).astype(F32)

    def biases_out():
        bias_own[...] = jnp.zeros(bias_own.shape, F32)
        bias_own[0:3, 0:HC] = mm(qkvb_ref[...], place().astype(BF16))
        bias_own[3:4, pl.ds(pl.multiple_of(h * D, 128), D)] = param(6)
        for dz in (entry, z1, far):
            send(bias_own, biases.at[h], bias_r + h, (w, dz), home, bias_sent)

        @pl.when(home)
        def _():
            biases[h] = bias_own[...]

        @pl.when(h == 0)
        def _():
            x[pl.ds(2 * R, R), :] = jnp.zeros((R, D), BF16)

    gain1, shift1 = param(0), param(1)

    def norm_block(b):
        def step(i):
            r = rows(R * b + i * C, C)
            normed, _inv = norm_stats(x[r, :].astype(F32))
            a1[r, :] = (normed * gain1 + shift1).astype(BF16)

        loop(0, R // C, step)

    def masks():
        bs_copy.wait()
        pick = (t == c).astype(jnp.int32)
        bl = bs_own[0:1, :] * pick + bs_buf[0:1, :] * (1 - pick)
        bl = jnp.concatenate([bl, bl], axis=1)

        def block_of(v):
            return jnp.where(
                bl == 4,
                lax.shift_right_logical(v, 2),
                jnp.where(bl == 8, lax.shift_right_logical(v, 3), lax.shift_right_logical(v, 4)),
            )

        key_no = block_of(lax.broadcasted_iota(jnp.int32, (T, 2 * T), 0))
        row_no = block_of(lax.rem(lax.broadcasted_iota(jnp.int32, (T, 2 * T), 1), T))
        m_same[...] = jnp.where(key_no == row_no, 0.0, NEG)
        m_lt[...] = jnp.where(key_no < row_no, 0.0, NEG)
        m_le[...] = jnp.where(key_no <= row_no, 0.0, NEG)

    def norm_local():
        tok_local()
        for k in range(2):
            recv(block(x, 1 - c, k), tok_r + 2 * (1 - c) + k, away)
        norm_block(t)

    takes_halo = jnp.logical_and(c == 1, h == 1)
    feeds = jnp.logical_and(c == 1, z == 1)

    def halo_pass(k):
        recv(block(x, 2, k), tok_r + 4 + k, takes_halo)
        send(block(x, 2, k), block(x, 1, k), tok_r + 2 + k, (w, 0), feeds)
        send(block(x, 2, k), block(x, 2, k), tok_r + 4 + k, (wc, z), takes_halo)

    def tokens_pass(k):
        recv(block(x, c, k), tok_r + 2 * c + k, away)
        send(block(x, c, k), block(x, c, k), tok_r + 2 * c + k, (wc, z), away)

    cot_r = take(recvs, 4)
    cot_local = []

    def cotangents_out(k):
        src = cot_ref.at[halves[k]]
        send(src, block(cot, c, k), cot_r + 2 * c + k, (wc, z), home)
        send(src, block(cot, 1 - c, k), cot_r + 2 * (1 - c) + k, (wc, z2), away)
        cot_local.append(local(src, block(cot, c, k), home))

    def norm_other():
        for k in range(2):
            recv(block(x, 1 - c, k), tok_r + 2 * (1 - c) + k, home)
        norm_block(1 - t)

    def norm_halo():
        for k in range(2):
            recv(block(x, 2, k), tok_r + 4 + k, jnp.logical_and(c == 0, h == 1))
        norm_block(2)

    def biases_in():
        recv(biases.at[0], bias_r, foreign(0))
        recv(biases.at[1], bias_r + 1, foreign(1))
        sent(bias_sent)
        bias_own[...] = biases[0] + biases[1]


    def wq(j):
        return w_q[3 * j : 3 * j + 3].reshape(HC, D)

    def cos_sin(place, n):
        r = rows(place, n)
        return cos_ref[r, :], sin_ref[r, :]

    def project(i, halo):
        r = rows(i * C, C)
        a = a1[r, :]
        place = (i * C - 2 * R) if halo else (R * h + lax.rem(i * C, R))
        cs, sn = cos_sin(place, C)
        if not halo:
            qv = mm_nt(a, wq(0)) + bias_own[0:1, :HC]
            for p in range(NP):
                v = qv[:, p * 128 : p * 128 + 128]
                qs[p, r, :] = ((v * cs + swap_halves(v) * sn) * 0.125).astype(BF16)
        kv = mm_nt(a, wq(1)) + bias_own[1:2, :HC]
        for p in range(NP):
            v = kv[:, p * 128 : p * 128 + 128]
            ks[p, r, :] = (v * cs + swap_halves(v) * sn).astype(BF16)
        vv = mm_nt(a, wq(2)) + bias_own[2:3, :HC]
        for p in range(NP):
            vs[p, r, :] = vv[:, p * 128 : p * 128 + 128].astype(BF16)

    def project_block(b):
        loop(0, HB, lambda i: project(HB * b + i, False))

    def project_halo():
        loop(NC, NC + HB, lambda i: project(i, True))

    halo_bias = jnp.where(h == 1, 0.0, NEG).astype(F32)
    lane = lax.broadcasted_iota(jnp.int32, (1, 128), 1)
    lo_f = (lane < 64).astype(F32)
    lo_mask = lo_f.astype(BF16)
    hi_mask = (1.0 - lo_f).astype(BF16)

    def both_heads(v):
        return jnp.concatenate([v * lo_mask, v * hi_mask], axis=0)

    def one_of_each(v):
        return v[:T] * lo_f + v[T:] * (1.0 - lo_f)

    def key_parts(b, i):
        parts = []
        if b == 0:
            parts.append((T * i, T, m_same))
        if i > 0:
            parts.append((R, T * i, None))
        parts.append((R + T * i, T, m_lt if b == 0 else m_le))
        parts.append((2 * R, R, halo_bias))
        return parts

    def scores_of(p, part, qm):
        start, n, mask = part
        sc = mm_nt(ks[p, pl.ds(start, n), :], qm)
        return sc if mask is None or mask is halo_bias else sc + mask[...]

    def bias_of(part):
        return halo_bias if part[2] is halo_bias else 0.0

    chunks = [(b, i) for b in range(2) for i in range(R // T)]

    def attend(p, n):
        if n == 0:
            turned[...] = vs[p].T
        for b, i in chunks[n : n + 1]:
            r = pl.ds(R * b + T * i, T)
            qm = both_heads(qs[p, r, :])
            parts = key_parts(b, i)
            sc = [scores_of(p, part, qm) for part in parts]
            top = None
            for part, v in zip(parts, sc):
                m = jnp.max(v, axis=0, keepdims=True) + bias_of(part)
                top = m if top is None else jnp.maximum(top, m)
            total, out = None, None
            for part, v in zip(parts, sc):
                e = jnp.exp(v - (top - bias_of(part)))
                l = jnp.sum(e, axis=0, keepdims=True)
                o = mm(turned[:, pl.ds(part[0], part[1])], e.astype(BF16))
                total = l if total is None else total + l
                out = o if out is None else out + o
            out = out / total
            att[p, r, :] = one_of_each(out.T).astype(BF16)
            lse[p, n] = top + jnp.log(total)

    e1_r = take(recvs, 4)
    e1_s = take(sends, 4)
    def swap_out(i, dst, si, ri):
        r = rows(i * C, C)
        remote(e1s.at[r], dst.at[r], si + i, ri + i, (wc, z)).start()

    def swap_in(i, dst, ri):
        r = rows(i * C, C)
        remote(dst.at[r], dst.at[r], 0, ri + i, (wc, z)).wait_recv()

    def swap_done(i, dst, si):
        r = rows(i * C, C)
        remote(e1s.at[r], dst.at[r], si + i, 0, (wc, z)).wait_send()

    def pairs(ref, r):
        return jnp.concatenate([ref[p, r, :] for p in range(NP)], axis=1)

    def out_project(i):
        r = rows(i * C, C)
        e1s[r, :] = mm(pairs(att, r), w_o[...].reshape(HC, D)).astype(BF16)
        swap_out(i, e1r, e1_s, e1_r)


    def clear():
        sm[...] = jnp.zeros(sm.shape, F32)
        ub[...] = jnp.zeros(ub.shape, F32)
        qb[...] = jnp.zeros(qb.shape, F32)

    out_bias, gain2, shift2, down_bias = param(2), param(3), param(4), param(5)
    KG = float(np.sqrt(2.0 / np.pi))

    def wu(s):
        return jnp.concatenate([w_u[0, s].reshape(D // 2, D), w_u[1, s].reshape(D // 2, D)], axis=0)

    def wd(s):
        return jnp.concatenate([w_d[0, s].reshape(D // 2, D), w_d[1, s].reshape(D // 2, D)], axis=0)

    def feed(i):
        r = rows(i * C, C)
        swap_in(i, e1r, e1_r)
        hv = x[r, :].astype(F32) + e1s[r, :].astype(F32) + e1r[r, :].astype(F32) + out_bias
        hid[r, :] = hv
        normed, _inv = norm_stats(hv)
        act = (normed * gain2 + shift2).astype(BF16)
        a2[r, :] = act
        for s in range(2):
            cols = pl.ds(s * D, D)
            u = mm(act, wu(s)) + bias_own[3:4, s * D : (s + 1) * D]
            u2 = u * u
            th = jnp.tanh(KG * u * (1.0 + 0.044715 * u2))
            half = 0.5 * (1.0 + th)
            gelu[r, cols] = (u * half).astype(BF16)
            slope = half + 0.5 * u * (1.0 - th * th) * (KG * (1.0 + 3 * 0.044715 * u2))
            gp[r, cols] = slope.astype(BF16)

    def cot_pass(k):
        cot_local[k]()
        recv(block(cot, c, k), cot_r + 2 * c + k, away)
        send(block(cot, c, k), block(cot, c, k), cot_r + 2 * c + k, (wc, z), away)

    def cot_in():
        for k in range(2):
            recv(block(cot, 1 - c, k), cot_r + 2 * (1 - c) + k)

    ra_r = {g: take(recvs, 2) for g, _, _ in RED}
    rb_r = {g: take(recvs, 2) for g, _, _ in RED}
    rc_r = {g: take(recvs, 2) for g, _, _ in RED}
    rd_r = {g: take(recvs, 2) for g, _, _ in RED}
    fin_r = {g: take(recvs, 3) for g, _, _ in RED}
    pass_r = take(recvs, 2)
    fin_local = {}
    size = {g: (n, r) for g, n, r in RED}
    turn = {g: k % 2 for k, (g, _, _) in enumerate(RED)}

    def add(dst, src):
        dst[...] = (dst[...].astype(F32) + src[...].astype(F32)).astype(BF16)

    def reduce_a(g):
        send(G[g].at[:, 0, :, 1 - xx], RA[g].at[0], ra_r[g], (wx, z))
        send(G[g].at[:, 1, 1 - yy, :], RA[g].at[1], ra_r[g] + 1, (wy, z))

    def reduce_b(g):
        n, r = size[g]
        recv(RA[g].at[0], ra_r[g])
        for k in range(n):
            add(G[g].at[k, 0, 1 - yy, xx], RA[g].at[0, k, 1 - yy])
        send(G[g].at[:, 0, 1 - yy, xx], RB[g].at[0], rb_r[g], (wy, z))
        recv(RA[g].at[1], ra_r[g] + 1)
        for k in range(n):
            add(G[g].at[k, 1, yy, 1 - xx], RA[g].at[1, k, 1 - xx])
        send(G[g].at[:, 1, yy, 1 - xx], RB[g].at[1], rb_r[g] + 1, (wx, z))
        for k in range(n):
            add(G[g].at[k, 0, yy, xx], RA[g].at[0, k, yy])
            add(G[g].at[k, 1, yy, xx], RA[g].at[1, k, xx])

    def reduce_c(g):
        n, r = size[g]
        for s in range(2):
            recv(RB[g].at[s], rb_r[g] + s)
            for k in range(n):
                add(G[g].at[k, s, yy, xx], RB[g].at[s, k])
            piece = G[g].at[:, s, yy, xx]
            if g in DIRECT:
                at = (w, 2 * c + s)
                send(piece, RC[g].at[0], rc_r[g], at, is_far)
                send(piece, RD[g].at[1], rd_r[g] + 1, at, is_entry)
            else:
                send(piece, RC[g].at[s], rc_r[g] + s, (w, entry), is_far)
            send(piece, RD[g].at[0], rd_r[g], (w, z1), jnp.logical_and(home, h == 1 - s))

    def reduce_d(g):
        n, r = size[g]
        if g in DIRECT:
            return
        for s in range(2):
            recv(RC[g].at[s], rc_r[g] + s, is_entry)

            @pl.when(is_entry)
            def _():
                for k in range(n):
                    add(G[g].at[k, s, yy, xx], RC[g].at[s, k])

            send(G[g].at[:, s, yy, xx], RD[g].at[1], rd_r[g] + 1, (w, 2 * c + s), is_entry)

    def reduce_e(g):
        n, r = size[g]
        recv(RD[g].at[0], rd_r[g], home)
        recv(RD[g].at[1], rd_r[g] + 1, home)
        if g in DIRECT:
            recv(RC[g].at[0], rc_r[g], home)

        @pl.when(home)
        def _():
            for k in range(n):
                dst = G[g].at[k, h, yy, xx]
                v = dst[...].astype(F32) + RD[g][0, k].astype(F32) + RD[g][1, k].astype(F32)
                if g in DIRECT:
                    v = v + RC[g][0, k].astype(F32)
                dst[...] = v.astype(BF16)

        piece = G[g].at[:, h, yy, xx]
        out = FIN[g].at[:, yy, xx]
        fin_local[g] = local(piece, out, home)
        for j, dev in enumerate((wx, wy)):
            send(piece, out, fin_r[g] + j, (dev, z), home)
        send(piece, out, pass_r + int(g in (O, Q0, Q1, Q2)), (wc, z), home)

    def reduce_f(g):
        for j, (py, px) in enumerate(((yy, 1 - xx), (1 - yy, xx))):
            piece = FIN[g].at[:, py, px]
            recv(piece, fin_r[g] + j, home)
            if j == turn[g]:
                send(piece, piece, fin_r[g] + 2, ((wy, wx)[j], z), home)
            send(piece, piece, pass_r + int(g in (O, Q0, Q1, Q2)), (wc, z), home)

    def reduce_g(g):
        piece = FIN[g].at[:, 1 - yy, 1 - xx]
        recv(piece, fin_r[g] + 2, home)
        send(piece, piece, pass_r + int(g in (O, Q0, Q1, Q2)), (wc, z), home)

    def results_in():
        for g, _, _ in RED:
            fin_local[g]()
        for k, n in enumerate((2 * D, D)):
            recv(x.at[pl.ds(0, n)], pass_r + k, away)

    def grad_down(half, s):
        cols = pl.ds(pl.multiple_of(s * D + half * (D // 2), 128), D // 2)
        g = mm_tn(gelu[:, cols], cot[...])
        g_d[half, s] = g.astype(BF16).reshape(2, 2, 96, D)

    def grad_up(half, s):
        g = mm_tn(
            a2[:, half * (D // 2) : (half + 1) * (D // 2)],
            gp[:, pl.ds(pl.multiple_of(s * D, 128), D)],
        )
        w_u[half, s] = g.astype(BF16).reshape(2, 2, 96, D)

    def grads_down(half):
        loop(0, 2, lambda s: grad_down(half, s))

    def grads_up(half):
        sent(w_sent[U0 + half])
        loop(0, 2, lambda s: grad_up(half, s))

    e3_r, e3_s = take(recvs, 4), take(sends, 4)

    def back_up(i):
        r = rows(i * C, C)
        cv = cot[r, :]
        out = None
        for s in range(2):
            cols = pl.ds(s * D, D)
            gu = (mm_nt(cv, wd(s)) * gp[r, cols].astype(F32)).astype(BF16)
            gp[r, cols] = gu
            ub[0:1, cols] += jnp.sum(gu.astype(F32), axis=0, keepdims=True)
            o = mm_nt(gu, wu(s))
            out = o if out is None else out + o
        e1s[r, :] = out.astype(BF16)
        swap_out(i, e3r, e3_s, e3_r)

    def backs_up():
        loop(0, NC, lambda i: swap_done(i, e1r, e1_s))
        loop(0, NC, back_up)

    e2_r, e2_s = take(recvs, 2), take(sends, 2)

    def down_of(r):
        return mm(gelu[r, 0:D], wd(0)) + mm(gelu[r, D : 2 * D], wd(1))

    def down_other(i):
        r = rows(R * (1 - c) + i * C, C)
        d = rows(i * C, C)
        e2s[d, :] = down_of(r).astype(BF16)
        remote(e2s.at[d], e2r.at[d], e2_s + i, e2_r + i, (wc, z)).start()

    def down_own(i):
        r = rows(R * c + i * C, C)
        d = rows(i * C, C)
        part = down_of(r)
        remote(e2r.at[d], e2r.at[d], 0, e2_r + i, (wc, z)).wait_recv()
        y = hid[r, :] + part + e2r[d, :].astype(F32) + down_bias
        ybuf[d, :] = y.astype(BF16)
        sm[5:6, :] += jnp.sum(cot[r, :].astype(F32), axis=0, keepdims=True)

    z_orig = 2 * c + h
    y_r = take(recvs)
    y_local = []

    def down_mine():
        loop(0, HB, down_own)
        y_local.append(local(ybuf, act_out, home))
        send(ybuf, act_out, y_r, (wc, z_orig), away)

    def norm2_back(i):
        r = rows(i * C, C)
        swap_in(i, e3r, e3_r)
        g2 = e1s[r, :].astype(F32) + e3r[r, :].astype(F32)
        normed, inv = norm_stats(hid[r, :])
        gh = cot[r, :].astype(F32) + norm_back(g2, normed, inv, gain2)
        hid[r, :] = gh
        own = (lax.div(i, HB) == c).astype(F32)
        sm[3:4, :] += own * jnp.sum(g2 * normed, axis=0, keepdims=True)
        sm[4:5, :] += own * jnp.sum(g2, axis=0, keepdims=True)
        sm[2:3, :] += own * jnp.sum(gh, axis=0, keepdims=True)
        swap_done(i, e3r, e3_s)
        br = gh.astype(BF16)
        e1s[r, :] = br
        a2[r, 0:HC] = mm_nt(br, w_o[...].reshape(HC, D)).astype(BF16)

    def grad_out():
        everything = pl.ds(0, 2 * R)
        sent(w_sent[O])
        g_out = mm_tn(pairs(att, everything), e1s[...])
        w_o[...] = g_out.astype(BF16).reshape(3, 2, 2, 2, 16, D)

    def attend_back(p, n):
        if n == 0:
            dk[...] = jnp.zeros(dk.shape, F32)
            dv[...] = jnp.zeros(dv.shape, F32)
            turned[...] = ks[p].T
        for b, i in chunks[n : n + 1]:
            r = pl.ds(R * b + T * i, T)
            qm = both_heads(qs[p, r, :])
            ga = a2[r, p * 128 : p * 128 + 128]
            gm = both_heads(ga)
            parts = key_parts(b, i)
            log_total = lse[p, n]
            inner = (ga.astype(F32) * att[p, r, :].astype(F32)).T
            delta = jnp.concatenate(
                [
                    jnp.sum(inner[:HEAD_DIM], axis=0, keepdims=True),
                    jnp.sum(inner[HEAD_DIM:], axis=0, keepdims=True),
                ],
                axis=1,
            )
            dq = None
            for part in parts:
                k = pl.ds(part[0], part[1])
                pr = jnp.exp(scores_of(p, part, qm) - (log_total - bias_of(part)))
                ds = (pr * (mm_nt(vs[p, k, :], gm) - delta)).astype(BF16)
                dv[k, :] += mm(pr.astype(BF16), gm)
                dk[k, :] += mm(ds, qm)
                d = mm(turned[:, k], ds)
                dq = d if dq is None else dq + d
            dq = one_of_each(dq.T) * 0.125
            cs, sn = cos_sin(R * h + T * i, T)
            dq = (dq * cs - swap_halves(dq) * sn).astype(BF16)
            qs[p, r, :] = dq

    def attend_end(p):
        for b in range(3):
            cs, sn = cos_sin(R * h if b < 2 else 0, R)
            r = pl.ds(R * b, R)
            v = dk[r, :]
            ks[p, r, :] = (v * cs - swap_halves(v) * sn).astype(BF16)
            vs[p, r, :] = dv[r, :].astype(BF16)

    def grad_qkv(p):
        r, o = pl.ds(0, 2 * R), pl.ds(2 * R, R)
        lhs = jnp.concatenate([qs[p, r, :], ks[p, r, :], vs[p, r, :]], axis=1)
        over = jnp.concatenate([ks[p, o, :], vs[p, o, :]], axis=1)
        g = mm_tn(lhs, a1[r, :])
        g_over = mm_tn(over, a1[o, :])
        g_q[0, p] = g[:128].astype(BF16).reshape(2, 2, 2, 16, D)
        for j in range(2):
            part = g[128 * (j + 1) : 128 * (j + 2)] + g_over[128 * j : 128 * (j + 1)]
            g_q[j + 1, p] = part.astype(BF16).reshape(2, 2, 2, 16, D)
        cols = pl.ds(128 * p, 128)
        qb[0:1, cols] = jnp.sum(qs[p, r, :].astype(F32), axis=0, keepdims=True)
        qb[1:2, cols] = jnp.sum(ks[p].astype(F32), axis=0, keepdims=True)
        qb[2:3, cols] = jnp.sum(vs[p].astype(F32), axis=0, keepdims=True)

    def back_qkv(r, halo):
        g = mm(pairs(ks, r), wq(1)) + mm(pairs(vs, r), wq(2))
        return g if halo else g + mm(pairs(qs, r), wq(0))

    hal_r, hal_s = take(recvs, 2), take(sends, 2)
    halz_r = take(recvs, 2)
    e4_r, e4_s = take(recvs, 2), take(sends, 2)

    def halo_back(i):
        d = rows(i * C, C)
        hals[d, :] = back_qkv(rows(2 * R + i * C, C), True).astype(BF16)

        @pl.when(c == 0)
        def _():
            remote(hals.at[d], halr.at[d], hal_s + i, hal_r + i, (wc, z)).start()

    def halos_back():
        loop(0, HB, halo_back)

    def other_back(i):
        d = rows(i * C, C)
        e2s[d, :] = back_qkv(rows(R * (1 - c) + i * C, C), False).astype(BF16)
        remote(e2s.at[d], e4r.at[d], e4_s + i, e4_r + i, (wc, z)).start()

    def others_back():
        loop(0, HB, lambda i: remote(
            e2s.at[rows(i * C, C)], e2r.at[rows(i * C, C)], e2_s + i, 0, (wc, z)).wait_send())
        loop(0, HB, other_back)

    def halo_sum(k):
        d = pl.ds(k * C, C)
        recv(halr.at[d], hal_r + k, c == 1)

        @pl.when(c == 1)
        def _():
            add(hals.at[d], halr.at[d])

        send(hals.at[d], halz.at[d], halz_r + k, (w, z1), jnp.logical_and(c == 1, h == 1))

    def own_back(i):
        tg[rows(i * C, C), :] = back_qkv(rows(R * c + i * C, C), False)

    def owns_back():
        loop(0, HB, own_back)

        @pl.when(jnp.logical_not(gets))
        def _():
            halz[...] = jnp.zeros(halz.shape, BF16)

    gets = jnp.logical_and(c == 1, h == 0)
    t_r = take(recvs, 2)

    def norm1_back(i):
        d = pl.ds(i * C, C)
        r = rows(R * c + i * C, C)
        recv(halz.at[d], halz_r + i, gets)
        remote(e4r.at[d], e4r.at[d], 0, e4_r + i, (wc, z)).wait_recv()
        g1 = tg[d, :] + e4r[d, :].astype(F32) + halz[d, :].astype(F32)
        normed, inv = norm_stats(x[r, :].astype(F32))
        out = hid[r, :] + norm_back(g1, normed, inv, gain1)
        sm[0:1, :] += jnp.sum(g1 * normed, axis=0, keepdims=True)
        sm[1:2, :] += jnp.sum(g1, axis=0, keepdims=True)
        e1r[d, :] = out.astype(BF16)
        send(e1r.at[d], tgrad_out.at[d], t_r + i, (wc, z_orig), away)
        t_local.append(local(e1r.at[d], tgrad_out.at[d], home))

    t_local = []

    me = lax.rem(w, 8)
    base = w - me
    sm_r, sm2_r = take(recvs, 8), take(recvs, 4)

    def small_out_plane():
        cf = c.astype(F32)
        for j in range(3):
            sm[6 + j : 7 + j, 0:HC] = qb[j : j + 1, :] * (1.0 - cf)
            sm[6 + j : 7 + j, HC : 2 * HC] = qb[j : j + 1, :] * cf
        for s in range(2):
            sm[9 + s : 10 + s, :] = ub[0:1, s * D : (s + 1) * D] * (1.0 - cf)
            sm[11 + s : 12 + s, :] = ub[0:1, s * D : (s + 1) * D] * cf
        smr[me] = sm[...]
        for dev in plane:
            send(smr.at[me], smr.at[me], sm_r + me, dev)

    def small_out_z():
        for dev, _ in plane:
            other = dev - base
            recv(smr.at[other], sm_r + other)
        total = smr[0]
        for k in range(1, 8):
            total = total + smr[k]
        smz[z] = total
        for dev in (z1, z2, z3):
            send(smz.at[z], smz.at[z], sm2_r + z, (w, dev))

    def small_end():
        for dev in (z1, z2, z3):
            recv(smz.at[dev], sm2_r + dev)
        total = smz[0] + smz[1] + smz[2] + smz[3]
        sm[...] = total
        small_out[...] = total
        small_out[9:10, :] = sm[pl.ds(9 + z, 1), :]
        mine = sm[6:9, pl.ds(pl.multiple_of(HC * t, 128), HC)]
        small_out[6:9, 0 : HC // 2] = lax.dot_general(
            mine, place(), (((1,), (1,)), ((), ())), precision=lax.Precision.HIGHEST,
            preferred_element_type=F32,
        )

    weights_out(Q)
    biases_out()
    halo_out(0)
    tokens_out(0)
    halo_out(1)
    weights_spread(Q)
    halo_pass(0)
    tokens_out(1)
    tokens_pass(0)
    weights_out(O)
    tokens_home()
    weights_relay(Q)
    norm_local()
    weights_spread(O)
    masks()
    halo_pass(1)
    weights_out(U0)
    tokens_pass(1)
    weights_relay(O)
    weights_spread(U0)
    norm_halo()
    biases_in()
    weights_wait(Q)
    weights_out(U1)
    project_block(t)
    norm_other()
    weights_out(D0)
    project_block(1 - t)
    weights_spread(U1)
    project_halo()
    attend(0, 0)
    attend(0, 1)
    clear()
    cotangents_out(0)
    weights_wait(O)
    attend(0, 2)
    attend(0, 3)
    attend(0, 4)
    attend(0, 5)
    weights_relay(U0)
    attend(0, 6)
    weights_out(D1)
    attend(0, 7)
    attend(1, 0)
    attend(1, 1)
    attend(1, 2)
    attend(1, 3)
    weights_relay(U1)
    weights_spread(D0)
    attend(1, 4)
    attend(1, 5)
    attend(1, 6)
    attend(1, 7)
    attend(2, 0)
    attend(2, 1)
    attend(2, 2)
    cotangents_out(1)
    attend(2, 3)
    weights_wait(U0)
    attend(2, 4)
    attend(2, 5)
    attend(2, 6)
    weights_spread(D1)
    attend(2, 7)
    loop(0, NC, out_project)
    weights_relay(D0)
    weights_wait(U1)
    loop(0, NC, feed)
    weights_relay(D1)
    cot_pass(0)
    cot_pass(1)
    weights_wait(D0)
    cot_in()
    grads_down(0)
    weights_wait(D1)
    reduce_a(D0)
    loop(0, HB, down_other)
    grads_down(1)
    reduce_a(D1)
    backs_up()
    reduce_b(D0)
    grads_up(0)
    reduce_a(U0)
    down_mine()
    grads_up(1)
    loop(0, NC, norm2_back)
    attend_back(0, 0)
    reduce_a(U1)
    attend_back(0, 1)
    reduce_b(D1)
    attend_back(0, 2)
    attend_back(0, 3)
    attend_back(0, 4)
    attend_back(0, 5)
    reduce_c(D0)
    reduce_b(U0)
    attend_back(0, 6)
    attend_back(0, 7)
    attend_end(0)
    grad_out()
    attend_back(1, 0)
    reduce_a(O)
    attend_back(1, 1)
    reduce_c(D1)
    grad_qkv(0)
    attend_back(1, 2)
    attend_back(1, 3)
    attend_back(1, 4)
    reduce_b(U1)
    attend_back(1, 5)
    attend_back(1, 6)
    attend_back(1, 7)
    attend_end(1)
    attend_back(2, 0)
    reduce_b(O)
    reduce_d(D0)
    attend_back(2, 1)
    reduce_a(Q0)
    reduce_c(U1)
    attend_back(2, 2)
    grad_qkv(1)
    reduce_a(Q1)
    reduce_c(O)
    reduce_d(D1)
    attend_back(2, 3)
    reduce_e(D0)
    reduce_c(U0)
    attend_back(2, 4)
    attend_back(2, 5)
    attend_back(2, 6)
    attend_back(2, 7)
    attend_end(2)
    reduce_b(Q1)
    reduce_d(U1)
    reduce_b(Q0)
    halos_back()
    halo_sum(0)
    grad_qkv(2)
    reduce_e(U1)
    reduce_e(O)
    reduce_c(Q0)
    reduce_e(D1)
    halo_sum(1)
    reduce_a(Q2)
    reduce_c(Q1)
    reduce_f(O)
    others_back()
    reduce_d(U0)
    reduce_f(D0)
    reduce_b(Q2)
    reduce_e(Q0)
    reduce_g(D0)
    reduce_e(U0)
    reduce_e(Q1)
    owns_back()
    reduce_c(Q2)
    reduce_f(Q0)
    norm1_back(0)
    reduce_e(Q2)
    norm1_back(1)
    small_out_plane()
    reduce_f(Q1)
    reduce_f(Q2)
    reduce_g(O)
    reduce_g(Q0)
    reduce_g(Q2)
    reduce_f(D1)
    small_out_z()
    reduce_g(Q1)
    reduce_f(U0)
    reduce_f(U1)
    reduce_g(U0)
    reduce_g(D1)
    reduce_g(U1)
    small_end()
    results_in()
    recv(act_out, y_r, away)
    y_local[0]()
    for k in range(HB):
        d = pl.ds(k * C, C)
        recv(tgrad_out.at[d], t_r + k, away)
        t_local[k]()
    loop(0, HB, lambda i: remote(
        e2s.at[rows(i * C, C)], e4r.at[rows(i * C, C)], e4_s + i, 0, (wc, z)).wait_send())

    @pl.when(c == 0)
    def _():
        for k in range(HB):
            d = pl.ds(k * C, C)
            remote(hals.at[d], halr.at[d], hal_s + k, 0, (wc, z)).wait_send()

    sent(w_sent[Q])
    sent(w_sent[D0])
    sent(w_sent[D1])
    sent(pending)
    counts = (next(sends), next(recvs), next(locals_))
    assert counts[0] <= ss.shape[0] and counts[1] <= rs.shape[0] and counts[2] <= ls.shape[0], counts


def finish_kernel(
    small_ref, q_ref, o_ref, u_ref, d_ref, act_ref, tg_ref,
    g1, s1, ob, g2, s2, db, upb, qkvb, gq, go, gu, gd, act, tg,
    low, high, kept, flat, square, ls, ss, cs, vs,
):
    n = low.shape[1]
    parts = [
        (src.at[pl.ds(k, n)], dst.at[pl.ds(k, n)])
        for src, dst in ((u_ref, gu), (d_ref, gd), (o_ref, go), (q_ref, gq))
        for k in range(0, src.shape[0], n)
    ]
    loads = [pltpu.make_async_copy(a, low.at[k], ls.at[k]) for k, (a, _) in enumerate(parts)]
    stores = [pltpu.make_async_copy(high.at[k], b, ss.at[k]) for k, (_, b) in enumerate(parts)]
    inward = [pltpu.make_async_copy(a, kept.at[k], cs.at[k]) for k, a in enumerate((act_ref, tg_ref))]
    outward = [pltpu.make_async_copy(kept.at[k], b, cs.at[2 + k]) for k, b in enumerate((act, tg))]
    for load in loads + inward:
        load.start()
    for v, k in zip(flat, (0, 1, 2, 3, 4, 5, 9)):
        v[...] = small_ref[k, :]
    square[...] = small_ref[6:9, : qkvb.shape[1]]
    vectors = [
        pltpu.make_async_copy(v, out, vs.at[k])
        for k, (v, out) in enumerate(zip((*flat, square), (g1, s1, ob, g2, s2, db, upb, qkvb)))
    ]
    for copy in vectors:
        copy.start()
    for k, load in enumerate(loads):
        load.wait()
        high[k] = low[k].astype(F32)
        stores[k].start()
    for load, store in zip(inward, outward):
        load.wait()
        store.start()
    for copy in stores + outward + vectors:
        copy.wait()


def finish(small, fq, fo, fu, fd, act, tgrad):
    n, D = fo.shape
    steps = (fq.shape[0] + fo.shape[0] + fu.shape[0] + fd.shape[0]) // n
    anyspec = pl.BlockSpec(memory_space=pl.ANY)
    vspec = pl.BlockSpec(memory_space=pltpu.VMEM)
    sds = jax.ShapeDtypeStruct
    return pl.pallas_call(
        finish_kernel,
        out_shape=[sds((D,), F32)] * 7 + [sds((3, n), F32)]
        + [sds(v.shape, F32) for v in (fq, fo, fu, fd)]
        + [sds(v.shape, v.dtype) for v in (act, tgrad)],
        in_specs=[vspec] + [anyspec] * 6,
        out_specs=[anyspec] * 14,
        scratch_shapes=[
            pltpu.VMEM((steps, n, D), BF16),
            pltpu.VMEM((steps, n, D), F32),
            pltpu.VMEM((2, *act.shape), BF16),
            [pltpu.VMEM((D,), F32)] * 7,
            pltpu.VMEM((3, n), F32),
            pltpu.SemaphoreType.DMA((steps,)),
            pltpu.SemaphoreType.DMA((steps,)),
            pltpu.SemaphoreType.DMA((4,)),
            pltpu.SemaphoreType.DMA((8,)),
        ],
        compiler_params=pltpu.CompilerParams(vmem_limit_bytes=61 * 1024 * 1024),
        name="finish",
    )(small, fq, fo, fu, fd, act, tgrad)


def shards(
    tokens, block_size, ln1_gain, ln1_shift, qkv_weight, qkv_bias, out_weight, out_bias,
    ln2_gain, ln2_shift, up_weight, up_bias, down_weight, down_bias, cotangent, groups,
):
    R, D = tokens.shape
    local_width = qkv_weight.shape[2]
    HC = 2 * local_width
    FC = 2 * up_weight.shape[1]
    cos, sin = tables(2 * R)
    wq = jnp.transpose(qkv_weight, (1, 2, 0)).reshape(9, 2, 2, 16, D)
    wo = out_weight.reshape(3, 2, 2, 16, D)
    wu = up_weight.reshape(2, 2, 2, 96, D)
    wdn = down_weight.reshape(2, 2, 2, 96, D)
    anyspec = pl.BlockSpec(memory_space=pl.ANY)
    vspec = pl.BlockSpec(memory_space=pltpu.VMEM)
    sds = jax.ShapeDtypeStruct
    fins = [sds((3, 3, 2, 2, 16, D), BF16), sds((3, 2, 2, 16, D), BF16)]
    fins += [sds((2, 2, 2, 96, D), BF16)] * 2
    V = pltpu.VMEM
    weights = [V((n, 2, 2, 2, r, D), BF16) for n, r in ((9, 16), (3, 16), (2, 96), (2, 96))]
    recvs = []
    for _, n, r in RED:
        recvs += [
            V((2, n, 2, r, D), BF16),
            V((2, n, r, D), BF16),
            V((2, n, r, D), BF16),
            V((2, n, r, D), BF16),
        ]
    NP = HC // 128
    outs = pl.pallas_call(
        layer_kernel,
        out_shape=[sds((R, D), BF16), sds((R, D), BF16), sds((16, D), F32)] + fins,
        in_specs=[vspec] * 10 + [pl.BlockSpec(memory_space=pltpu.SMEM)] + [anyspec] * 6,
        out_specs=[anyspec, anyspec, vspec] + [anyspec] * 4,
        scratch_shapes=[
            V((3 * R, D), BF16),
            V((3 * R, D), BF16),
            V((NP, 2 * R, 128), BF16),
            V((NP, 3 * R, 128), BF16),
            V((NP, 3 * R, 128), BF16),
            V((NP, 2 * R, 128), BF16),
            V((NP, 2 * R // T, 1, 2 * T), F32),
            V((2 * R, D), F32),
            V((2 * R, D), BF16),
            V((2 * R, FC), BF16),
            V((2 * R, FC), BF16),
            V((2 * R, D), BF16),
            *weights,
            V((3, 3, 2, 2, 2, 16, D), BF16),
            V((2, 2, 2, 2, 96, D), BF16),
            V((8, FC), F32),
            V((2, 8, FC), F32),
            V((8, 128), jnp.int32),
            V((8, 128), jnp.int32),
            V((T, 2 * T), F32),
            V((T, 2 * T), F32),
            V((T, 2 * T), F32),
            V((128, 3 * R), BF16),
            V((2 * R, D), BF16),
            V((2 * R, D), BF16),
            V((R, D), BF16),
            V((R, D), BF16),
            V((2 * R, D), BF16),
            V((R, D), BF16),
            V((R, D), BF16),
            V((R, D), BF16),
            V((R, D), BF16),
            V((R, D), BF16),
            V((R, D), F32),
            V((3 * R, 128), F32),
            V((3 * R, 128), F32),
            *recvs,
            V((16, D), F32),
            V((8, 16, D), F32),
            V((4, 16, D), F32),
            V((8, FC), F32),
            V((8, HC), F32),
            pltpu.SemaphoreType.DMA((260,)),
            pltpu.SemaphoreType.DMA((220,)),
            pltpu.SemaphoreType.DMA((24,)),
        ],
        compiler_params=pltpu.CompilerParams(
            collective_id=0, has_side_effects=True, vmem_limit_bytes=62 * 1024 * 1024
        ),
        name="layer",
    )(
        jnp.asarray(cos), jnp.asarray(sin), ln1_gain, ln1_shift, out_bias, ln2_gain, ln2_shift,
        down_bias, up_bias, qkv_bias, block_size, tokens, cotangent, wq, wo, wu, wdn,
    )
    act, tgrad, small, fq, fo, fu, fd = outs
    if groups > 1:
        ids = [[g * 8 + k for g in range(groups)] for k in range(8)]
        small = lax.psum(small, "wide", axis_index_groups=ids)
    g1, s1, ob, g2, s2, db, upb, qkvb, gq, go, gu, gd, act, tgrad = finish(
        small, fq.reshape(3 * local_width, D), fo.reshape(local_width, D), fu.reshape(D, D),
        fd.reshape(D, D), act, tgrad,
    )
    if groups > 1:
        gq, go, gu, gd = lax.psum((gq, go, gu, gd), "wide", axis_index_groups=ids)
    gq = jnp.transpose(gq.reshape(3, local_width, D), (2, 0, 1))
    return act, tgrad, g1, s1, gq, qkvb, go, ob, g2, s2, gu, upb, gd, db


def solution(mesh):
    both = P(("wide", "narrow"), None)
    in_specs = (
        both, P("wide"), P(), P(), P(None, None, "narrow"), P(None, "narrow"), P("narrow", None), P(),
        P(), P(), P(None, "narrow"), P("narrow"), P("narrow", None), P(), both,
    )
    out_specs = (
        both, both, P(), P(), P(None, None, "narrow"), P(None, "narrow"), P("narrow", None), P(),
        P(), P(), P(None, "narrow"), P("narrow"), P("narrow", None), P(),
    )
    groups = mesh.shape["wide"] // 8

    def body(*args):
        return shards(*args, groups)

    return jax.shard_map(body, mesh=mesh, in_specs=in_specs, out_specs=out_specs, check_vma=False)
```
